32 devices in a mesh: dp: 4 (over x, core), blk: 8 (over z, y).
Axes of the slice: x: 2, y: 2, z: 4, core: 2. Of those that a mesh axis runs over, the one named last changes fastest.
Arguments:
- hidden: bfloat16 [8, 3, 1024, 1024], P('dp', None, 'blk'), may hold values from -6 to 6
- encoder: bfloat16 [8, 1024, 1024], P('dp', 'blk'), may hold values from -6 to 6
- lengths: int32 [8, 8], P('dp'), may hold values from 0 to 1024, as said below
- qkv_self: float32 [3, 1024, 1024], P(None, 'dp'), may hold values from -0.1875 to 0.1875
- out_self: float32 [1024, 1024], P('dp'), may hold values from -0.75 to 0.75
- rel_table: float32 [16, 32], replicated, may hold values from -4 to 4
- qkv_cross: float32 [3, 1024, 1024], P(None, 'dp'), may hold values from -0.1875 to 0.1875
- out_cross: float32 [1024, 1024], P('dp'), may hold values from -0.75 to 0.75
- ffn_in: float32 [1024, 4096], P('dp'), may hold values from -0.1875 to 0.1875
- ffn_out: float32 [4096, 1024], P('dp'), may hold values from -0.09375 to 0.09375
- norm_gain: float32 [3, 1024], replicated, may hold values from 0.5 to 1.5
- norm_bias: float32 [3, 1024], replicated, may hold values from -3 to 3
- cotangent: bfloat16 [8, 3, 1024, 1024], P('dp', None, 'blk'), may hold values from -6 to 6
Outputs:
- output: bfloat16 [8, 3, 1024, 1024], P('dp', None, 'blk')
- d_hidden: float32 [8, 3, 1024, 1024], P('dp', None, 'blk')
- d_encoder: float32 [8, 1024, 1024], P('dp', 'blk')
- g_qkv_self: float32 [3, 1024, 1024], P(None, ('dp', 'blk'))
- g_out_self: float32 [1024, 1024], P(('dp', 'blk'))
- g_rel_table: float32 [16, 32], replicated
- g_qkv_cross: float32 [3, 1024, 1024], P(None, ('dp', 'blk'))
- g_out_cross: float32 [1024, 1024], P(('dp', 'blk'))
- g_ffn_in: float32 [1024, 4096], P(('dp', 'blk'))
- g_ffn_out: float32 [4096, 1024], P(('dp', 'blk'))
- g_norm_gain: float32 [3, 1024], replicated
- g_norm_bias: float32 [3, 1024], replicated
The draws below stay inside these ranges and needn't reach their ends.
Inputs may be any that keep to these rules, and one draw needn't show every extreme that they name: `lengths`: each row sums to 1024, nonzero entries first. In each group of 2 streams of one index of dp, one stream, drawn from the seed, is a single document of 1024 positions; the other streams hold documents of 128, 256 and 512 positions.
All inputs are finite; a program needn't handle non-finite values.
Results may differ from the reference program's by a relative error of at most 0.025.
The reference program's roundings to bfloat16 on the way count: a program that leaves them out, or rounds other values in their place, can miss the bound.
Values may be sent and summed in bfloat16 or wider, within the bound.
No kernel may reach another device: no remote copies, remote signals or barrier semaphores. Data moves between devices by JAX's collectives and lax.ppermute only.
A program may use at most 576 MiB of HBM per device.

```python
import math
import jax
import jax.numpy as jnp
from jax import lax

D = 1024
H = 16
HD = 64
FF = 4096
BUCKETS = 32
STR_DEV = 2
DOCS = 8
SLEN = 1024
STREAMS = 8


def draw_lengths(key, part):
    key = jax.random.fold_in(key, 11)
    pick_key, form_key = jax.random.split(key, 2)
    forms = jnp.array([[4, 2, 1, 1, 0, 0, 0, 0], [2, 4, 2, 0, 0, 0, 0, 0], [1, 1, 2, 4, 0, 0, 0, 0], [2, 2, 4, 0, 0, 0, 0, 0], [4, 4, 0, 0, 0, 0, 0, 0], [1, 2, 1, 4, 0, 0, 0, 0], [2, 1, 1, 2, 2, 0, 0, 0], [4, 1, 1, 2, 0, 0, 0, 0], [1, 4, 2, 1, 0, 0, 0, 0], [2, 2, 2, 2, 0, 0, 0, 0], [1, 1, 4, 1, 1, 0, 0, 0]], jnp.int32)
    forms = jnp.pad(forms, ((0, 0), (0, DOCS - 8)))
    picked = jax.random.randint(form_key, (STREAMS,), 0, forms.shape[0]).astype(jnp.int32)
    ragged = forms[picked] * (SLEN // 8)
    spanning = jnp.concatenate([jnp.full((STREAMS, 1), SLEN, jnp.int32), jnp.zeros((STREAMS, DOCS - 1), jnp.int32)], axis=1)
    chosen = jax.random.randint(pick_key, (STREAMS // STR_DEV,), 0, STR_DEV).astype(jnp.int32)
    slots = jnp.arange(STREAMS, dtype=jnp.int32)
    flagged = slots % STR_DEV == jnp.repeat(chosen, STR_DEV)
    return jnp.where(flagged[:, None], spanning, ragged).astype(jnp.int32)


def level_of(own_key, extent, cuts, least, top_value):
    def one(axis_at, parts):
        steps = jax.random.uniform(jax.random.fold_in(jax.random.fold_in(own_key, 6), axis_at), (parts,), jnp.float32, least / len(cuts), top_value / len(cuts))
        return jnp.repeat(jnp.exp(steps), extent[axis_at] // parts).reshape((-1,) + (1,) * (len(extent) - axis_at - 1))

    gain = one(*cuts[0])
    for cut in cuts[1:]:
        gain = gain * one(*cut)
    return gain


def normal_values(key, extent, spread, most, cuts=(), held_as=jnp.bfloat16):
    values = jax.random.normal(key, extent, jnp.float32) * spread
    if len(cuts) > 0:
        values = level_of(key, extent, cuts, -0.22, 0.18) * values
    return jnp.clip(values, min=-most, max=most).astype(held_as)


def setup_inputs(seed: int = 0) -> dict:
    key_of = jax.random.split(jax.random.key(seed), 14)
    return {
        "hidden": normal_values(key_of[0], (STREAMS, 3, SLEN, D), 1.0, 6.0, ((0, 4), (2, 8))),
        "encoder": normal_values(key_of[1], (STREAMS, SLEN, D), 1.0, 6.0, ((0, 4), (1, 8))),
        "lengths": draw_lengths(jax.random.fold_in(key_of[13], 71), 0),
        "qkv_self": normal_values(key_of[3], (3, D, D), D ** -0.5, 0.1875, ((1, 4),), jnp.float32),
        "out_self": normal_values(key_of[4], (D, D), (D // 16) ** -0.5, 0.75, ((0, 4),), jnp.float32),
        "rel_table": normal_values(key_of[5], (H, BUCKETS), 1.0, 4.0, (), jnp.float32),
        "qkv_cross": normal_values(key_of[6], (3, D, D), D ** -0.5, 0.1875, ((1, 4),), jnp.float32),
        "out_cross": normal_values(key_of[7], (D, D), (D // 16) ** -0.5, 0.75, ((0, 4),), jnp.float32),
        "ffn_in": normal_values(key_of[8], (D, FF), D ** -0.5, 0.1875, ((0, 4),), jnp.float32),
        "ffn_out": normal_values(key_of[9], (FF, D), FF ** -0.5, 0.09375, ((0, 4),), jnp.float32),
        "norm_gain": jnp.clip(1.0 + 0.1 * jax.random.normal(key_of[10], (3, D), jnp.float32), 0.5, 1.5),
        "norm_bias": normal_values(key_of[11], (3, D), 0.5, 3.0, (), jnp.float32),
        "cotangent": normal_values(key_of[12], (STREAMS, 3, SLEN, D), 1.0, 6.0, ((0, 4), (2, 8))),
    }


highest = lax.Precision.HIGHEST
bucket_edges = tuple((math.ceil(16 * 8 ** (power / 16)) for power in range(1, 16)))

@jax.custom_vjp
def low(v):
    return lax.optimization_barrier(v.astype(jnp.bfloat16)).astype(jnp.float32)

@jax.custom_vjp
def low_back(v):
    return v

def low_keep(v):
    return (low(v), None)

def low_pass(kept, grad):
    return (grad,)

def back_keep(v):
    return (v, None)

def back_low(kept, grad):
    return (low(grad),)
low.defvjp(low_keep, low_pass)
low_back.defvjp(back_keep, back_low)

def segments_of(lengths, length_all):
    doc_ends = jnp.cumsum(lengths, axis=-1)
    places = jnp.arange(length_all, dtype=jnp.int32)
    return lax.optimization_barrier(jnp.sum((places[None, :, None] >= doc_ends[:, None, :]).astype(jnp.int32), axis=-1))

def bucket_of(distance):
    nearby = jnp.maximum(distance, 0)
    distant = 16 + sum(((nearby >= edge).astype(jnp.int32) for edge in bucket_edges))
    return jnp.where(nearby < 16, nearby, distant)

def layer_norm(values_in, gain_row, bias_row):
    centred = values_in - lax.optimization_barrier(jnp.mean(values_in, axis=-1, keepdims=True))
    inv_scale = lax.rsqrt(lax.optimization_barrier(jnp.mean(centred * centred, axis=-1, keepdims=True)) + 1e-05)
    return centred * inv_scale * gain_row + bias_row

def dense(low_input, weight):
    return low_back(jnp.dot(low_input, low(weight), precision=highest))

def self_attend(query_all, key_all, value_all, segment, rel_table):
    block_rows = math.gcd(SLEN, 512)
    places = jnp.arange(SLEN, dtype=jnp.int32)
    streams_ok = (jnp.arange(3) > 0)[:, None, None]

    def one_block(begin_at):
        query_rows = begin_at + jnp.arange(block_rows, dtype=jnp.int32)
        query_part = lax.dynamic_slice_in_dim(query_all, begin_at, block_rows, 1)
        key_part = lax.dynamic_slice_in_dim(key_all, begin_at, block_rows, 1)
        value_part = lax.dynamic_slice_in_dim(value_all, begin_at, block_rows, 1)
        same_doc = lax.dynamic_slice_in_dim(segment, begin_at, block_rows, 0)[:, None] == segment[None, :]
        distance = query_rows[:, None] - places[None, :]
        table_bias = jnp.take(rel_table, bucket_of(distance), axis=1)
        main_scores = low_back(jnp.einsum('clhe,she->chls', query_part, key_all[0], precision=highest) * 0.125 + table_bias[None])
        own_scores = low_back(jnp.einsum('clhe,clhe->chl', query_part, key_part, precision=highest) * 0.125 + rel_table[:, 0][None, :, None])
        later = same_doc & (distance > 0)
        allowed = jnp.stack([same_doc & (distance >= 0), later, later])[:, None]
        main_scores = jnp.where(allowed, main_scores, -1e+30)
        own_scores = jnp.where(streams_ok, own_scores, -1e+30)
        row_max = jnp.maximum(lax.optimization_barrier(jnp.max(main_scores, axis=-1)), own_scores)
        main_exp = jnp.exp(main_scores - row_max[..., None])
        own_exp = jnp.exp(own_scores - row_max)
        row_total = lax.optimization_barrier(jnp.sum(main_exp, axis=-1)) + own_exp
        main_prob = low(main_exp / row_total[..., None])
        own_prob = low(own_exp / row_total)
        mixture = jnp.einsum('chls,she->clhe', main_prob, value_all[0], precision=highest)
        return mixture + jnp.transpose(own_prob, (0, 2, 1))[..., None] * value_part
    starts = jnp.arange(0, SLEN, block_rows, dtype=jnp.int32)
    pieces = lax.map(jax.checkpoint(one_block), starts)
    return jnp.transpose(pieces, (1, 0, 2, 3, 4)).reshape(query_all.shape)

def cross_attend(query_all, key_enc, value_enc, segment):
    block_rows = math.gcd(SLEN, 512)

    def one_block(begin_at):
        query_part = lax.dynamic_slice_in_dim(query_all, begin_at, block_rows, 1)
        same_doc = lax.dynamic_slice_in_dim(segment, begin_at, block_rows, 0)[:, None] == segment[None, :]
        scores = low_back(jnp.einsum('clhe,she->chls', query_part, key_enc, precision=highest) * 0.125)
        scores = jnp.where(same_doc[None, None], scores, -1e+30)
        row_max = lax.optimization_barrier(jnp.max(scores, axis=-1, keepdims=True))
        exps = jnp.exp(scores - row_max)
        probs = low(exps / lax.optimization_barrier(jnp.sum(exps, axis=-1, keepdims=True)))
        return jnp.einsum('chls,she->clhe', probs, value_enc, precision=highest)
    starts = jnp.arange(0, SLEN, block_rows, dtype=jnp.int32)
    pieces = lax.map(jax.checkpoint(one_block), starts)
    return jnp.transpose(pieces, (1, 0, 2, 3, 4)).reshape(query_all.shape)

def stream_forward(hidden_part, encoder_part, segment, weights):
    qkv_self, out_self, rel_table, qkv_cross, out_cross, ffn_in, ffn_out, norm_gain, norm_bias = weights
    heads_shape = (3, SLEN, H, HD)
    hidden_low = low(hidden_part)
    query_all = low(dense(hidden_low, qkv_self[0])).reshape(heads_shape)
    key_all = low(dense(hidden_low, qkv_self[1])).reshape(heads_shape)
    value_all = low(dense(hidden_low, qkv_self[2])).reshape(heads_shape)
    attended = low(low_back(self_attend(query_all, key_all, value_all, segment, rel_table).reshape(3, SLEN, D)))
    first_out = layer_norm(hidden_part + dense(attended, out_self), norm_gain[0], norm_bias[0])
    encoder_low = low(encoder_part)
    cross_query = low(dense(low(first_out), qkv_cross[0])).reshape(heads_shape)
    cross_key = low(dense(encoder_low, qkv_cross[1])).reshape(SLEN, H, HD)
    cross_value = low(dense(encoder_low, qkv_cross[2])).reshape(SLEN, H, HD)
    cross_att = low(low_back(cross_attend(cross_query, cross_key, cross_value, segment).reshape(3, SLEN, D)))
    second_out = layer_norm(first_out + dense(cross_att, out_cross), norm_gain[1], norm_bias[1])
    inner_act = dense(low(second_out), ffn_in)
    activated = low(jax.nn.gelu(inner_act, approximate=False))
    return layer_norm(second_out + dense(activated, ffn_out), norm_gain[2], norm_bias[2])

def reference(hidden, encoder, lengths, qkv_self, out_self, rel_table, qkv_cross, out_cross, ffn_in, ffn_out, norm_gain, norm_bias, cotangent):
    segments = segments_of(lengths, SLEN)
    params = (qkv_self, out_self, rel_table, qkv_cross, out_cross, ffn_in, ffn_out, norm_gain, norm_bias)

    def forward(hidden_all, encoder_all, weights):

        def per_stream(packed):
            return stream_forward(packed[0], packed[1], packed[2], weights)
        return lax.map(per_stream, (hidden_all, encoder_all, segments))
    result, pullback = jax.vjp(forward, hidden.astype(jnp.float32), encoder.astype(jnp.float32), params)
    grad_hidden, grad_encoder, grads = pullback(cotangent.astype(jnp.float32))
    return (result.astype(jnp.bfloat16), grad_hidden, grad_encoder, grads[0], grads[1], grads[2], grads[3], grads[4], grads[5], grads[6], grads[7], grads[8])
```

```python
from functools import partial
import math
import jax
import jax.numpy as jnp
from jax import lax
from jax.experimental import pallas as pl
from jax.experimental.pallas import tpu as pltpu
from jax.sharding import PartitionSpec as P

bucket_edges = tuple((math.ceil(16 * 8 ** (power / 16)) for power in range(1, 16)))
score_unit = 0.125 * math.log2(math.e)
masked_out = -1e30


def fold_rows(values_in, combine):
    return combine(values_in.reshape(values_in.shape[0] // 8, 8, values_in.shape[1]), axis=0)


def two_heads(tile, half):
    wide = tile.astype(jnp.float32)
    low_lanes = lax.broadcasted_iota(jnp.int32, wide.shape, 1) < half
    tall = jnp.concatenate([jnp.where(low_lanes, wide, 0.0), jnp.where(low_lanes, 0.0, wide)], axis=0)
    return tall.astype(jnp.bfloat16)


def turned_twice(tile):
    return jnp.concatenate([tile.astype(jnp.float32)] * 2, axis=0).T


def join_heads(tall, half):
    rows = tall.shape[0] // 2
    low_lanes = lax.broadcasted_iota(jnp.int32, (rows, tall.shape[1]), 1) < half
    return jnp.where(low_lanes, tall[:rows], tall[rows:])


def dot_00(left_side, right_side):
    return lax.dot_general(left_side, right_side, (((0,), (0,)), ((), ())), preferred_element_type=jnp.float32)


def dot_10(left_side, right_side):
    return lax.dot_general(left_side, right_side, (((1,), (0,)), ((), ())), preferred_element_type=jnp.float32)


def slot_of(place, block, blocks):
    gap = place ^ block
    return (gap >> 1) + (blocks // 2) * (gap & 1)


def tile_of(bounds_ref, stream, block, near_tiles):
    first, place = bounds_ref[stream, 0], bounds_ref[stream, 1]
    gap = place - block
    outside = (block < first) | (gap < 0)
    plain = jnp.where(outside, near_tiles + 2, jnp.minimum(gap, near_tiles) + 1)
    return jnp.where(gap == 0, 0, plain), plain


def shift_of(bounds_ref, stream, block):
    inside = (block >= bounds_ref[stream, 0]) & (block <= bounds_ref[stream, 1])
    return jnp.where(inside, 0.0, masked_out)


def forward_kernel(is_self, rows, near_tiles, *refs):
    if is_self:
        bounds_ref, q_ref, k_ref, v_ref, ko_ref, vo_ref, bias_ref, own_bias_ref, o_ref, lse_ref, score_ref, total_ref = refs
    else:
        bounds_ref, q_ref, k_ref, v_ref, o_ref, lse_ref, score_ref, total_ref = refs
    stream = pl.program_id(1)
    half = q_ref.shape[3] // 2
    wide = 2 * rows
    first_chunk = bounds_ref[stream, 0] // 2
    past_chunk = bounds_ref[stream, 1] // 2 + 1
    place, blocks = bounds_ref[stream, 2], k_ref.shape[0]
    q_turned = [two_heads(q_ref[0, c], half).T for c in range(3)]

    def score_step(chunk, tops):
        tops = list(tops)
        for part in range(2):
            block = 2 * chunk + part
            key_rows = pl.ds(pl.multiple_of(block * rows, rows), rows)
            keys = k_ref[slot_of(place, block, blocks), 0]
            if is_self:
                diag_tile, plain_tile = tile_of(bounds_ref, stream, block, near_tiles)
                later_tile = jnp.where(diag_tile == 0, 1, plain_tile)
                tile_index = (jnp.where(diag_tile == 0, 0, plain_tile), later_tile, later_tile)
            for c in range(3):
                scores = dot_10(keys, q_turned[c])
                if is_self:
                    scores = scores + bias_ref[0, tile_index[c]]
                else:
                    scores = scores + shift_of(bounds_ref, stream, block)
                score_ref[key_rows, pl.ds(c * wide, wide)] = scores
                tops[c] = jnp.maximum(tops[c], fold_rows(scores, jnp.max))
        return tuple(tops)

    tops = lax.fori_loop(
        first_chunk, past_chunk, score_step, tuple((jnp.full((8, wide), masked_out, jnp.float32) for _ in range(3)))
    )
    row_top = [jnp.max(tops[c], axis=0, keepdims=True) for c in range(3)]
    if is_self:
        own_turned = [None] + [turned_twice(ko_ref[0, c]) for c in range(2)]
        own_score = [None] + [
            jnp.sum(q_turned[c].astype(jnp.float32) * own_turned[c], axis=0, keepdims=True)
            + own_bias_ref[0]
            for c in (1, 2)
        ]
        row_top = [row_top[0]] + [jnp.maximum(row_top[c], own_score[c]) for c in (1, 2)]
    total_ref[...] = jnp.zeros_like(total_ref)

    def value_step(chunk, sums):
        sums = list(sums)
        chunk_rows = pl.ds(pl.multiple_of(chunk * wide, wide), wide)
        values = jnp.concatenate(
            [v_ref[slot_of(place, 2 * chunk + part, blocks), 0] for part in range(2)], axis=0
        )
        for c in range(3):
            lanes = pl.ds(c * wide, wide)
            weights = jnp.exp2((score_ref[chunk_rows, lanes] - row_top[c]) * score_unit)
            sums[c] = sums[c] + fold_rows(weights, jnp.sum)
            total_ref[:, lanes] += dot_00(values, weights.astype(jnp.bfloat16))
        return tuple(sums)

    sums = lax.fori_loop(
        first_chunk, past_chunk, value_step, tuple((jnp.zeros((8, wide), jnp.float32) for _ in range(3)))
    )
    for c in range(3):
        row_sum = jnp.sum(sums[c], axis=0, keepdims=True)
        mixed = total_ref[:, c * wide : (c + 1) * wide]
        if is_self and c > 0:
            own_weight = jnp.exp2((own_score[c] - row_top[c]) * score_unit)
            row_sum = row_sum + own_weight
            value_turned = turned_twice(vo_ref[0, c - 1])
            mixed = mixed + own_weight * value_turned
        mixed = mixed / row_sum
        o_ref[0, c] = join_heads(mixed.T, half).astype(jnp.bfloat16)
        lse_ref[0, 0, :, c * wide : (c + 1) * wide] = row_top[c] * score_unit + jnp.log2(row_sum)


def backward_kernel(is_self, rows, near_tiles, *refs):
    if is_self:
        (bounds_ref, q_ref, k_ref, v_ref, o_ref, do_ref, lse_ref, ko_ref, vo_ref, bias_ref, own_bias_ref,
         dq_ref, dk_ref, dv_ref, dko_ref, dvo_ref, tiles_ref, own_sum_ref, prob_ref, grad_ref, total_ref) = refs
    else:
        (bounds_ref, q_ref, k_ref, v_ref, o_ref, do_ref, lse_ref,
         dq_ref, dk_ref, dv_ref, prob_ref, grad_ref, total_ref) = refs
    stream = pl.program_id(1)
    half = q_ref.shape[3] // 2
    wide = 2 * rows
    first_chunk = bounds_ref[stream, 0] // 2
    past_chunk = bounds_ref[stream, 1] // 2 + 1
    place, blocks = bounds_ref[stream, 2], k_ref.shape[0]
    chunk_count = blocks // 2
    q_tall = [two_heads(q_ref[0, c], half) for c in range(3)]
    do_tall = [two_heads(do_ref[0, c], half) for c in range(3)]
    q_turned = [tall.T for tall in q_tall]
    do_turned = [tall.T for tall in do_tall]
    lse = [lse_ref[0, 0, :, c * wide : (c + 1) * wide] for c in range(3)]
    centre = []
    for c in range(3):
        o_turned = turned_twice(o_ref[0, c])
        centre.append(jnp.sum(do_turned[c].astype(jnp.float32) * o_turned, axis=0, keepdims=True))
    q_all = jnp.concatenate(q_tall, axis=0)
    do_all = jnp.concatenate(do_tall, axis=0)
    total_ref[...] = jnp.zeros_like(total_ref)

    if is_self:

        @pl.when(stream == 0)
        def _():
            tiles_ref[...] = jnp.zeros_like(tiles_ref)
            own_sum_ref[...] = jnp.zeros_like(own_sum_ref)

    def blank_step(chunk, carry):
        for part in range(2):
            slot = slot_of(place, 2 * chunk + part, blocks)
            dk_ref[slot, 0] = jnp.zeros((rows, 2 * half), jnp.bfloat16)
            dv_ref[slot, 0] = jnp.zeros((rows, 2 * half), jnp.bfloat16)
        return carry

    lax.fori_loop(0, first_chunk, blank_step, 0)
    lax.fori_loop(past_chunk, chunk_count, blank_step, 0)

    def chunk_step(chunk, carry):
        for part in range(2):
            block = 2 * chunk + part
            part_rows = pl.ds(part * rows, rows)
            keys = k_ref[slot_of(place, block, blocks), 0]
            values = v_ref[slot_of(place, block, blocks), 0]
            if is_self:
                diag_tile, plain_tile = tile_of(bounds_ref, stream, block, near_tiles)
                later_tile = jnp.where(diag_tile == 0, 1, plain_tile)
                tile_index = (jnp.where(diag_tile == 0, 0, plain_tile), later_tile, later_tile)
            grad_sum = None
            for c in range(3):
                lanes = pl.ds(c * wide, wide)
                scores = dot_10(keys, q_turned[c])
                if is_self:
                    scores = scores + bias_ref[0, tile_index[c]]
                else:
                    scores = scores + shift_of(bounds_ref, stream, block)
                probs = jnp.exp2(scores * score_unit - lse[c])
                prob_ref[part_rows, lanes] = probs.astype(jnp.bfloat16)
                grads = probs * (dot_10(values, do_turned[c]) - centre[c])
                grad_ref[part_rows, lanes] = grads.astype(jnp.bfloat16)
                if is_self:
                    grad_sum = grads if grad_sum is None else grad_sum + grads
            if is_self:
                tiles_ref[0, tile_index[1]] += grad_sum
        slots = [slot_of(place, 2 * chunk + part, blocks) for part in range(2)]
        value_grads = dot_10(prob_ref[...], do_all).astype(jnp.bfloat16)
        key_grads = (0.125 * dot_10(grad_ref[...], q_all)).astype(jnp.bfloat16)
        for part in range(2):
            dv_ref[slots[part], 0] = value_grads[part * rows : (part + 1) * rows]
            dk_ref[slots[part], 0] = key_grads[part * rows : (part + 1) * rows]
        total_ref[...] += dot_00(jnp.concatenate([k_ref[slot, 0] for slot in slots], axis=0), grad_ref[...])
        return carry

    lax.fori_loop(first_chunk, past_chunk, chunk_step, 0)
    for c in range(3):
        turned = total_ref[:, c * wide : (c + 1) * wide]
        if is_self and c > 0:
            own_turned = turned_twice(ko_ref[0, c - 1])
            value_turned = turned_twice(vo_ref[0, c - 1])
            q_wide = q_turned[c].astype(jnp.float32)
            do_wide = do_turned[c].astype(jnp.float32)
            own_score = jnp.sum(q_wide * own_turned, axis=0, keepdims=True) + own_bias_ref[0]
            own_prob = jnp.exp2(own_score * score_unit - lse[c])
            own_dp = jnp.sum(do_wide * value_turned, axis=0, keepdims=True)
            own_grad = own_prob * (own_dp - centre[c])
            own_sum_ref[0] += own_grad
            own_grad = own_grad.astype(jnp.bfloat16).astype(jnp.float32)
            own_low = own_prob.astype(jnp.bfloat16).astype(jnp.float32)
            turned = turned + own_grad * own_turned
            dko = (0.125 * own_grad * q_wide).T
            dko_ref[0, c - 1] = (dko[:rows] + dko[rows:]).astype(jnp.bfloat16)
            dvo = (own_low * do_wide).T
            dvo_ref[0, c - 1] = (dvo[:rows] + dvo[rows:]).astype(jnp.bfloat16)
        dq_ref[0, c] = (0.125 * join_heads(turned.T, half)).astype(jnp.bfloat16)


def attend_forward(bounds, query, keys, values, own=None, near_tiles=0, head_size=64):
    streams, _, rows, width = query.shape
    blocks = keys.shape[0]
    length = blocks * rows
    lanes = 2 * head_size
    pairs = width // lanes
    is_self = own is not None
    row_spec = pl.BlockSpec((1, 3, rows, lanes), lambda p, n, s: (n, 0, 0, p))
    key_spec = pl.BlockSpec((blocks, 1, rows, lanes), lambda p, n, s: (0, n, 0, p))
    in_specs = [row_spec, key_spec, key_spec]
    args = [query, keys, values]
    if is_self:
        own_keys, own_values, tiles, own_bias = own
        own_spec = pl.BlockSpec((1, 2, rows, lanes), lambda p, n, s: (n, 0, 0, p))
        in_specs += [
            own_spec,
            own_spec,
            pl.BlockSpec((1,) + tiles.shape[1:], lambda p, n, s: (p, 0, 0, 0)),
            pl.BlockSpec((1, 1, 2 * rows), lambda p, n, s: (p, 0, 0)),
        ]
        args += [own_keys, own_values, tiles, own_bias]
    flops = 2 * 2 * streams * 3 * rows * length * width
    return pl.pallas_call(
        partial(forward_kernel, is_self, rows, near_tiles),
        grid_spec=pltpu.PrefetchScalarGridSpec(
            num_scalar_prefetch=1,
            grid=(pairs, streams),
            in_specs=in_specs,
            out_specs=[row_spec, pl.BlockSpec((1, 1, 1, 6 * rows), lambda p, n, s: (p, n, 0, 0))],
            scratch_shapes=[
                pltpu.VMEM((length, 6 * rows), jnp.float32),
                pltpu.VMEM((lanes, 6 * rows), jnp.float32),
            ],
        ),
        out_shape=[
            jax.ShapeDtypeStruct(query.shape, jnp.bfloat16),
            jax.ShapeDtypeStruct((pairs, streams, 1, 6 * rows), jnp.float32),
        ],
        compiler_params=pltpu.CompilerParams(vmem_limit_bytes=20 * 1024 * 1024),
        cost_estimate=pl.CostEstimate(flops=4 * flops, bytes_accessed=20_000_000, transcendentals=0),
    )(bounds, *args)


def attend_backward(bounds, query, keys, values, mixed, mix_grad, lse, own=None, near_tiles=0, head_size=64):
    streams, _, rows, width = query.shape
    blocks = keys.shape[0]
    length = blocks * rows
    lanes = 2 * head_size
    pairs = width // lanes
    is_self = own is not None
    row_spec = pl.BlockSpec((1, 3, rows, lanes), lambda p, n, s: (n, 0, 0, p))
    key_spec = pl.BlockSpec((blocks, 1, rows, lanes), lambda p, n, s: (0, n, 0, p))
    in_specs = [row_spec, key_spec, key_spec, row_spec, row_spec,
                pl.BlockSpec((1, 1, 1, 6 * rows), lambda p, n, s: (p, n, 0, 0))]
    args = [query, keys, values, mixed, mix_grad, lse]
    out_specs = [row_spec, key_spec, key_spec]
    out_shape = [jax.ShapeDtypeStruct(query.shape, jnp.bfloat16)] + [jax.ShapeDtypeStruct(keys.shape, jnp.bfloat16)] * 2
    if is_self:
        own_keys, own_values, tiles, own_bias = own
        own_spec = pl.BlockSpec((1, 2, rows, lanes), lambda p, n, s: (n, 0, 0, p))
        tile_spec = pl.BlockSpec((1,) + tiles.shape[1:], lambda p, n, s: (p, 0, 0, 0))
        own_bias_spec = pl.BlockSpec((1, 1, 2 * rows), lambda p, n, s: (p, 0, 0))
        in_specs += [own_spec, own_spec, tile_spec, own_bias_spec]
        args += [own_keys, own_values, tiles, own_bias]
        out_specs += [own_spec, own_spec, tile_spec, own_bias_spec]
        out_shape += [jax.ShapeDtypeStruct(own_keys.shape, jnp.bfloat16)] * 2
        out_shape += [jax.ShapeDtypeStruct(tiles.shape, jnp.float32), jax.ShapeDtypeStruct(own_bias.shape, jnp.float32)]
    flops = 5 * 2 * streams * 3 * rows * length * width
    return pl.pallas_call(
        partial(backward_kernel, is_self, rows, near_tiles),
        grid_spec=pltpu.PrefetchScalarGridSpec(
            num_scalar_prefetch=1,
            grid=(pairs, streams),
            in_specs=in_specs,
            out_specs=out_specs,
            scratch_shapes=[
                pltpu.VMEM((2 * rows, 6 * rows), jnp.bfloat16),
                pltpu.VMEM((2 * rows, 6 * rows), jnp.bfloat16),
                pltpu.VMEM((lanes, 6 * rows), jnp.float32),
            ],
        ),
        out_shape=out_shape,
        compiler_params=pltpu.CompilerParams(vmem_limit_bytes=20 * 1024 * 1024),
        cost_estimate=pl.CostEstimate(flops=4 * flops, bytes_accessed=40_000_000, transcendentals=0),
    )(bounds, *args)


def bucket_of(distance):
    nearby = jnp.maximum(distance, 0)
    distant = 16 + sum(((nearby >= edge).astype(jnp.int32) for edge in bucket_edges))
    return jnp.where(nearby < 16, nearby, distant)


def near_count(rows):
    gap = 1
    while rows * gap - (rows - 1) < bucket_edges[-1]:
        gap += 1
    return gap


def bias_tiles(rel_table, rows):
    heads, buckets = rel_table.shape
    near_tiles = near_count(rows)
    places = jnp.arange(rows, dtype=jnp.int32)
    distance = places[None, None, :] - places[None, :, None] + rows * jnp.arange(near_tiles, dtype=jnp.int32)[:, None, None]
    onehot = (bucket_of(distance)[..., None] == jnp.arange(buckets, dtype=jnp.int32)).astype(jnp.float32)
    shifted = 8.0 * (rel_table - rel_table[:, buckets - 1 :])
    gap = jnp.tile(places[None, :] - places[:, None], (1, 2))[None, None]
    near = jnp.concatenate(
        [
            jnp.einsum("dstk,pk->pdst", onehot, shifted[side::2], precision=lax.Precision.HIGHEST)
            for side in range(2)
        ],
        axis=-1,
    )
    diag = near[:, :1]
    tiles = jnp.concatenate(
        [
            jnp.where(gap >= 0, diag, masked_out),
            jnp.where(gap > 0, diag, masked_out),
            near[:, 1:],
            jnp.zeros_like(diag),
            jnp.full_like(diag, masked_out),
        ],
        axis=1,
    )
    own_bias = jnp.repeat(shifted[:, 0], rows).reshape(heads // 2, 1, 2 * rows)
    return tiles, own_bias, onehot


def table_grad(tile_grads, own_sums, onehot, bucket_count):
    pairs, tile_count, rows, wide = tile_grads.shape
    near_tiles = tile_count - 3
    sides = (tile_grads[..., : wide // 2], tile_grads[..., wide // 2 :])
    near_part, far_part = (
        jnp.stack(parts, axis=1)
        for parts in zip(
            *(
                (
                    jnp.einsum(
                        "pdst,dstk->pk", side[:, 1 : 1 + near_tiles], onehot, precision=lax.Precision.HIGHEST
                    ),
                    jnp.sum(side[:, 1 + near_tiles], axis=(1, 2)),
                )
                for side in sides
            )
        )
    )
    own_part = jnp.sum(own_sums.reshape(pairs, 2, wide // 2), axis=-1)
    buckets = jnp.arange(bucket_count)
    result = near_part + far_part[..., None] * (buckets == bucket_count - 1) + own_part[..., None] * (buckets == 0)
    return result.reshape(2 * pairs, bucket_count)


def norm_parts(values_in):
    centred = values_in - jnp.mean(values_in, axis=-1, keepdims=True)
    inv_scale = lax.rsqrt(jnp.mean(centred * centred, axis=-1, keepdims=True) + 1e-05)
    return (centred * inv_scale, inv_scale)


def norm_back(grad_in, normed, inv_scale, gain_row):
    scaled = grad_in * gain_row
    return inv_scale * (
        scaled
        - jnp.mean(scaled, axis=-1, keepdims=True)
        - normed * jnp.mean(scaled * normed, axis=-1, keepdims=True)
    )


def matmul(left_side, right_side):
    return jnp.einsum("...i,ij->...j", left_side, right_side, preferred_element_type=jnp.float32)


def matmul_t(left_side, right_side):
    return jnp.einsum("...j,ij->...i", left_side, right_side, preferred_element_type=jnp.float32)


def swap_core(values_in):
    size = lax.axis_size("dp")
    return lax.ppermute(values_in, "dp", [(i, i ^ 1) for i in range(size)])


def swap_chip(values_in):
    size = lax.axis_size("dp")
    return lax.ppermute(values_in, "dp", [(i, i ^ 2) for i in range(size)])


def swap_block(values_in, bit):
    size = lax.axis_size("blk")
    return lax.ppermute(values_in, "blk", [(i, i ^ bit) for i in range(size)])


def tie(value, *earlier):
    return lax.optimization_barrier((value,) + earlier)[0]


def assemble(pieces):
    count = pieces[0].shape[0]
    place = lax.axis_index("dp")
    split_rows = len(pieces) > 4

    def ordered(at, row):
        def joined(*parts):
            shards = [[parts[0]], [parts[1]]]
            if split_rows:
                halves = (parts[2:4], parts[4:6])
                shards += [[half[row], half[1 - row]] for half in halves]
            else:
                shards += [[parts[2]], [parts[3]]]
            return [
                jnp.concatenate([part[k] for index in range(4) for part in shards[at ^ index]], axis=0)
                for k in range(count)
            ]

        return joined

    if split_rows:
        row = lax.axis_index("blk") % 2
        return lax.switch(2 * place + row, [ordered(at, r) for at in range(4) for r in range(2)], *pieces)
    return lax.switch(place, [ordered(at, 0) for at in range(4)], *pieces)


def half_rows(shard):
    rows = shard.shape[1] // 2
    return lax.dynamic_slice_in_dim(shard, (lax.axis_index("blk") % 2) * rows, rows, 1)


def outer_low(left_side, right_side):
    return jnp.einsum("ni,nj->ij", left_side, right_side, preferred_element_type=jnp.float32)


def pick(values_in, index, axis):
    return lax.dynamic_index_in_dim(values_in, index, axis, keepdims=False)


def add_low(kept, arrived):
    return (kept.astype(jnp.float32) + arrived.astype(jnp.float32)).astype(jnp.bfloat16)


def open_core(grads):
    core = lax.axis_index("dp") % 2
    blocks = lax.axis_size("blk")

    def split(core_at):
        return jnp.stack(
            [pick(g.reshape(2, 2, blocks, g.shape[0] // (4 * blocks), g.shape[1]), core_at, 1) for g in grads], axis=2
        )

    return split(1 - core), split(core)


def open_chip(values_in):
    chip = lax.axis_index("dp") // 2
    return pick(values_in, 1 - chip, 0), pick(values_in, chip, 0)


def open_block(values_in, axis, bit):
    shape = values_in.shape
    values_in = values_in.reshape(shape[:axis] + (shape[axis] // 2, 2) + shape[axis + 1 :])
    mine = (lax.axis_index("blk") // bit) % 2
    return pick(values_in, 1 - mine, axis + 1), pick(values_in, mine, axis + 1)


def start_rows(values_in):
    return [values_in] + [swap_block(values_in, gap) for gap in range(2, lax.axis_size("blk"), 2)]


def finish_rows(pieces):
    return jnp.stack(pieces + [swap_block(piece, 1) for piece in pieces])


def fold_odd(terms):
    half = terms.shape[0] // 2
    return terms[:half], swap_block(terms[half:], 1)


def fold_even(terms):
    return sum(
        [swap_block(terms[index], 2 * index).astype(jnp.float32) for index in range(1, terms.shape[0])],
        terms[0].astype(jnp.float32),
    )


def exchange_blocks(values_in):
    count = values_in.shape[0]
    mine = lax.axis_index("blk") // 2
    come = [swap_block(pick(values_in, mine ^ gap, 0), 2 * gap) for gap in range(1, count)]
    total = pick(values_in, mine, 0).astype(jnp.float32)
    for piece in come:
        total = total + piece.astype(jnp.float32)
    return total


def split_shares(share):
    share = share.astype(jnp.float32)
    return [share[k] for k in range(share.shape[0])]


def sum_everywhere(values_in):
    total = values_in + swap_core(values_in)
    total = total + swap_chip(total)
    total = total + swap_block(total, 1)
    blocks = lax.axis_size("blk")
    mine = lax.axis_index("blk") // 2
    come = jnp.stack([total] + [swap_block(total, 2 * gap) for gap in range(1, blocks // 2)])
    return sum(pick(come, mine ^ index, 0) for index in range(blocks // 2))


def shards(
    hidden,
    encoder,
    lengths,
    qkv_self,
    out_self,
    rel_table,
    qkv_cross,
    out_cross,
    ffn_in,
    ffn_out,
    norm_gain,
    norm_bias,
    cotangent,
):
    streams, _, rows, width = hidden.shape
    heads, buckets = rel_table.shape
    head_size = width // heads
    place = lax.axis_index("blk")
    main_rows = start_rows(hidden[:, 0])
    low = partial(lax.convert_element_type, new_dtype=jnp.bfloat16)
    qkv_low = low(qkv_self)
    middle_low = jnp.concatenate([low(out_self)[None], low(qkv_cross), low(out_cross)[None]])
    first_low_w, second_low_w = low(ffn_in)[None], low(ffn_out)[None]
    qkv_far = swap_chip(qkv_low)
    main_all = finish_rows(main_rows)
    w_qkv = assemble([qkv_low, swap_core(qkv_low), qkv_far, swap_core(qkv_far)])
    doc_ends = jnp.cumsum(lengths, axis=-1)
    begin = place * rows
    doc_begin = jnp.max(jnp.where(doc_ends <= begin, doc_ends, 0), axis=-1)
    doc_end = jnp.min(jnp.where(doc_ends > begin, doc_ends, rows * lax.axis_size("blk")), axis=-1)
    first_block = (doc_begin // rows).astype(jnp.int32)
    last_block = (doc_end // rows - 1).astype(jnp.int32)
    places = jnp.full_like(first_block, place)
    self_bounds = jnp.stack([first_block, places, places], axis=1)
    cross_bounds = jnp.stack([first_block, last_block, places], axis=1)
    near_tiles = near_count(rows)
    tiles, own_bias, onehot = bias_tiles(rel_table, rows)

    def flat(values_in):
        return values_in.reshape(-1, values_in.shape[-1])

    def tall(values_in):
        return values_in.reshape(streams, 3, rows, width)

    hidden_own = hidden[:, 1:]
    query = matmul(hidden, w_qkv[0]).astype(jnp.bfloat16)
    own_keys = matmul(hidden_own, w_qkv[1]).astype(jnp.bfloat16)
    own_values = matmul(hidden_own, w_qkv[2]).astype(jnp.bfloat16)
    middle_far = swap_chip(tie(middle_low, qkv_far))
    enc_all = finish_rows(start_rows(tie(encoder, main_all)))
    main_keys = matmul(main_all, w_qkv[1]).astype(jnp.bfloat16)
    main_values = matmul(main_all, w_qkv[2]).astype(jnp.bfloat16)
    own = (own_keys, own_values, tiles, own_bias)

    first_half_sent = half_rows(first_low_w)
    first_far = swap_chip(tie(first_half_sent, main_values, query))
    query = tie(query, first_half_sent)
    attended, self_lse = attend_forward(
        self_bounds, query, main_keys, main_values, own, near_tiles, head_size
    )
    second_half_sent = half_rows(second_low_w)
    second_far = swap_chip(tie(second_half_sent, attended, first_far))
    first_other = swap_block(tie(first_far, attended), 1)
    middle_pieces = [middle_low, swap_core(middle_low), middle_far, swap_core(tie(middle_far, attended))]
    w_out, *c_qkv, c_out = assemble(middle_pieces)
    first_norm, first_scale = norm_parts(
        flat(hidden).astype(jnp.float32) + matmul(flat(attended), w_out)
    )
    first_out = first_norm * norm_gain[0] + norm_bias[0]
    first_low = first_out.astype(jnp.bfloat16)
    cross_query = matmul(first_low, c_qkv[0]).astype(jnp.bfloat16)
    enc_keys = matmul(enc_all, c_qkv[1]).astype(jnp.bfloat16)
    enc_values = matmul(enc_all, c_qkv[2]).astype(jnp.bfloat16)
    cross_att, cross_lse = attend_forward(
        cross_bounds, tall(cross_query), enc_keys, enc_values, None, 0, head_size
    )
    second_other = swap_block(tie(second_far, cross_query), 1)
    w_first, w_second = (
        assemble(
            [shard, swap_core(shard), far, other, swap_core(far), swap_core(tie(other, cross_att))]
        )[0]
        for shard, far, other in (
            (first_low_w, first_far, first_other),
            (second_low_w, second_far, second_other),
        )
    )
    second_norm, second_scale = norm_parts(first_out + matmul(flat(cross_att), c_out))
    second_out = second_norm * norm_gain[1] + norm_bias[1]
    second_low = second_out.astype(jnp.bfloat16)
    inner_act = matmul(second_low, w_first)
    normal_cdf = 0.5 * (1.0 + lax.erf(inner_act * math.sqrt(0.5)))
    activated = (inner_act * normal_cdf).astype(jnp.bfloat16)
    density = jnp.exp(-0.5 * inner_act * inner_act) * (1.0 / math.sqrt(2.0 * math.pi))
    act_slope = (normal_cdf + inner_act * density).astype(jnp.bfloat16)
    third_norm, third_scale = norm_parts(second_out + matmul(activated, w_second))
    output = tall((third_norm * norm_gain[2] + norm_bias[2]).astype(jnp.bfloat16))

    grad_out = flat(cotangent).astype(jnp.float32)
    gain_three = jnp.sum(grad_out * third_norm, axis=0)
    bias_three = jnp.sum(grad_out, axis=0)
    third_grad = norm_back(grad_out, third_norm, third_scale, norm_gain[2])
    third_low = third_grad.astype(jnp.bfloat16)
    second_part = outer_low(activated, third_low).astype(jnp.bfloat16)
    second_sent, second_kept = open_core([second_part])
    second_come = swap_core(second_sent)
    inner_grad = (
        matmul_t(tie(third_low, second_sent), w_second) * act_slope.astype(jnp.float32)
    ).astype(jnp.bfloat16)
    chip_sent, chip_kept = open_chip(add_low(second_kept, second_come))
    chip_come = swap_chip(chip_sent)
    inner_grad = tie(inner_grad, chip_sent)
    first_part = outer_low(second_low, inner_grad).astype(jnp.bfloat16)
    first_sent, first_kept = open_core([first_part])
    first_come = swap_core(first_sent)
    second_total = third_grad + matmul_t(tie(inner_grad, first_sent), w_first)
    gain_two = jnp.sum(second_total * second_norm, axis=0)
    bias_two = jnp.sum(second_total, axis=0)
    second_grad = norm_back(second_total, second_norm, second_scale, norm_gain[1])
    cross_low = second_grad.astype(jnp.bfloat16)
    first_chip_sent, first_chip_kept = open_chip(add_low(first_kept, first_come))
    first_chip_come = swap_chip(first_chip_sent)
    cross_mix_grad = tall(matmul_t(tie(cross_low, first_chip_sent), c_out).astype(jnp.bfloat16))
    cross_query_grad, enc_key_grad, enc_value_grad = attend_backward(
        cross_bounds, tall(cross_query), enc_keys, enc_values, cross_att, cross_mix_grad, cross_lse,
        None, 0, head_size,
    )
    encoder_terms = (matmul_t(enc_key_grad, c_qkv[1]) + matmul_t(enc_value_grad, c_qkv[2])).astype(jnp.bfloat16)
    encoder_kept, encoder_come = fold_odd(encoder_terms)
    second_row_sent, second_row_kept = open_block(add_low(chip_kept, tie(chip_come, encoder_terms)), 0, 1)
    second_row_come = swap_block(second_row_sent, 1)
    first_row_sent, first_row_kept = open_block(add_low(first_chip_kept, tie(first_chip_come, second_row_sent)), 0, 1)
    first_row_come = swap_block(first_row_sent, 1)
    first_total = second_grad + matmul_t(flat(tie(cross_query_grad, first_row_sent)), c_qkv[0])
    gain_one = jnp.sum(first_total * first_norm, axis=0)
    bias_one = jnp.sum(first_total, axis=0)
    first_grad = norm_back(first_total, first_norm, first_scale, norm_gain[0])
    out_low = first_grad.astype(jnp.bfloat16)
    cross_parts = [
        outer_low(flat(left), flat(right)).astype(jnp.bfloat16)
        for left, right in (
            (cross_att, cross_low),
            (first_low, cross_query_grad),
            (enc_all, tie(enc_key_grad, out_low)),
            (enc_all, enc_value_grad),
            (attended, out_low),
        )
    ]
    cross_sent, cross_kept = open_core(cross_parts)
    cross_come = swap_core(cross_sent)
    mix_grad = tall(matmul_t(tie(out_low, cross_sent), w_out).astype(jnp.bfloat16))
    cross_chip_sent, cross_chip_kept = open_chip(add_low(cross_kept, tie(cross_come, mix_grad)))
    cross_chip_come = swap_chip(cross_chip_sent)
    second_half = add_low(second_row_kept, tie(second_row_come, mix_grad))
    first_half = add_low(first_row_kept, tie(first_row_come, mix_grad))
    g_second = exchange_blocks(second_half)[0]
    g_first = exchange_blocks(first_half)[0]
    encoder_half = add_low(encoder_kept, tie(encoder_come, second_half, first_half))
    d_encoder = fold_even(encoder_half)
    mix_grad = tie(mix_grad, cross_chip_sent, encoder_half)
    query_grad, key_grad, value_grad, own_key_grad, own_value_grad, tile_grads, own_sums = attend_backward(
        self_bounds, query, main_keys, main_values, attended, mix_grad, self_lse, own, near_tiles, head_size
    )
    main_terms = (matmul_t(key_grad, w_qkv[1]) + matmul_t(value_grad, w_qkv[2])).astype(jnp.bfloat16)
    main_kept, main_come = fold_odd(main_terms)
    cross_row_sent, cross_row_kept = open_block(add_low(cross_chip_kept, tie(cross_chip_come, main_terms)), 0, 1)
    cross_row_come = swap_block(cross_row_sent, 1)
    own_flat = flat(hidden_own)
    main_flat = flat(main_all)
    started = tie(query_grad, cross_row_sent)
    self_parts = [outer_low(flat(hidden), flat(started)).astype(jnp.bfloat16)] + [
        (outer_low(main_flat, flat(tie(grad, started))) + outer_low(own_flat, flat(own_grad))).astype(jnp.bfloat16)
        for grad, own_grad in ((key_grad, own_key_grad), (value_grad, own_value_grad))
    ]
    self_sent, self_kept = open_core(self_parts)
    self_come = swap_core(self_sent)
    local_grad = tall(first_grad) + matmul_t(tie(query_grad, self_sent), w_qkv[0])
    self_chip_sent, self_chip_kept = open_chip(add_low(self_kept, tie(self_come, local_grad)))
    self_chip_come = swap_chip(self_chip_sent)
    own_back = matmul_t(tie(own_key_grad, self_chip_sent), w_qkv[1]) + matmul_t(own_value_grad, w_qkv[2])
    main_half = add_low(main_kept, tie(main_come, own_back))
    main_back = fold_even(main_half)
    cross_share = exchange_blocks(add_low(cross_row_kept, tie(cross_row_come, own_back)))
    g_cross_out, *g_cross, g_self_out = split_shares(cross_share)
    g_cross = jnp.stack(g_cross)
    self_row_sent, self_row_kept = open_block(add_low(self_chip_kept, self_chip_come), 0, 1)
    self_row_come = swap_block(self_row_sent, 1)
    g_qkv = exchange_blocks(add_low(self_row_kept, self_row_come))
    d_hidden = local_grad + jnp.concatenate([main_back[:, None], own_back], axis=1)
    rel_grad = table_grad(tile_grads, own_sums, onehot, buckets)
    small = jnp.concatenate(
        [
            jnp.stack([gain_one, gain_two, gain_three, bias_one, bias_two, bias_three]),
            rel_grad.reshape(-1, width) if rel_grad.size % width == 0 else
            jnp.pad(rel_grad.reshape(1, -1), ((0, 0), (0, width - rel_grad.size))),
        ]
    )
    small = sum_everywhere(small)
    return (
        output,
        d_hidden,
        d_encoder,
        g_qkv,
        g_self_out,
        small[6:].reshape(-1)[: heads * buckets].reshape(heads, buckets),
        g_cross,
        g_cross_out,
        g_first,
        g_second,
        small[0:3],
        small[3:6],
    )


def solution(mesh):
    in_specs = (
        P("dp", None, "blk", None),
        P("dp", "blk", None),
        P("dp", None),
        P(None, "dp", None),
        P("dp", None),
        P(),
        P(None, "dp", None),
        P("dp", None),
        P("dp", None),
        P("dp", None),
        P(),
        P(),
        P("dp", None, "blk", None),
    )
    out_specs = (
        P("dp", None, "blk", None),
        P("dp", None, "blk", None),
        P("dp", "blk", None),
        P(None, ("dp", "blk"), None),
        P(("dp", "blk"), None),
        P(),
        P(None, ("dp", "blk"), None),
        P(("dp", "blk"), None),
        P(("dp", "blk"), None),
        P(("dp", "blk"), None),
        P(),
        P(),
    )
    return jax.shard_map(shards, mesh=mesh, in_specs=in_specs, out_specs=out_specs, check_vma=False)
```

```python
from functools import partial
import math
import jax
import jax.numpy as jnp
from jax import lax
from jax.experimental import pallas as pl
from jax.experimental.pallas import tpu as pltpu
from jax.sharding import PartitionSpec as P

bucket_edges = tuple((math.ceil(16 * 8 ** (power / 16)) for power in range(1, 16)))
score_unit = 0.125 * math.log2(math.e)
masked_out = -1e30


def fold_rows(values_in, combine):
    return combine(values_in.reshape(values_in.shape[0] // 8, 8, values_in.shape[1]), axis=0)


def two_heads(tile, half):
    wide = tile.astype(jnp.float32)
    low_lanes = lax.broadcasted_iota(jnp.int32, wide.shape, 1) < half
    tall = jnp.concatenate([jnp.where(low_lanes, wide, 0.0), jnp.where(low_lanes, 0.0, wide)], axis=0)
    return tall.astype(jnp.bfloat16)


def turned_twice(tile):
    return jnp.concatenate([tile.astype(jnp.float32)] * 2, axis=0).T


def join_heads(tall, half):
    rows = tall.shape[0] // 2
    low_lanes = lax.broadcasted_iota(jnp.int32, (rows, tall.shape[1]), 1) < half
    return jnp.where(low_lanes, tall[:rows], tall[rows:])


def dot_00(left_side, right_side):
    return lax.dot_general(left_side, right_side, (((0,), (0,)), ((), ())), preferred_element_type=jnp.float32)


def dot_10(left_side, right_side):
    return lax.dot_general(left_side, right_side, (((1,), (0,)), ((), ())), preferred_element_type=jnp.float32)


def slot_of(place, block, blocks):
    gap = place ^ block
    return (gap >> 1) + (blocks // 2) * (gap & 1)


def tile_of(bounds_ref, stream, block, near_tiles):
    first, place = bounds_ref[stream, 0], bounds_ref[stream, 1]
    gap = place - block
    outside = (block < first) | (gap < 0)
    plain = jnp.where(outside, near_tiles + 2, jnp.minimum(gap, near_tiles) + 1)
    return jnp.where(gap == 0, 0, plain), plain


def shift_of(bounds_ref, stream, block):
    inside = (block >= bounds_ref[stream, 0]) & (block <= bounds_ref[stream, 1])
    return jnp.where(inside, 0.0, masked_out)


def forward_kernel(is_self, rows, near_tiles, *refs):
    if is_self:
        bounds_ref, q_ref, k_ref, v_ref, ko_ref, vo_ref, bias_ref, own_bias_ref, o_ref, lse_ref, score_ref, total_ref = refs
    else:
        bounds_ref, q_ref, k_ref, v_ref, o_ref, lse_ref, score_ref, total_ref = refs
    stream = pl.program_id(1)
    half = q_ref.shape[3] // 2
    wide = 2 * rows
    first_chunk = bounds_ref[stream, 0] // 2
    past_chunk = bounds_ref[stream, 1] // 2 + 1
    place, blocks = bounds_ref[stream, 2], k_ref.shape[0]
    q_turned = [two_heads(q_ref[0, c], half).T for c in range(3)]

    def score_step(chunk, tops):
        tops = list(tops)
        for part in range(2):
            block = 2 * chunk + part
            key_rows = pl.ds(pl.multiple_of(block * rows, rows), rows)
            keys = k_ref[slot_of(place, block, blocks), 0]
            if is_self:
                diag_tile, plain_tile = tile_of(bounds_ref, stream, block, near_tiles)
                later_tile = jnp.where(diag_tile == 0, 1, plain_tile)
                tile_index = (jnp.where(diag_tile == 0, 0, plain_tile), later_tile, later_tile)
            for c in range(3):
                scores = dot_10(keys, q_turned[c])
                if is_self:
                    scores = scores + bias_ref[0, tile_index[c]]
                else:
                    scores = scores + shift_of(bounds_ref, stream, block)
                score_ref[key_rows, pl.ds(c * wide, wide)] = scores
                tops[c] = jnp.maximum(tops[c], fold_rows(scores, jnp.max))
        return tuple(tops)

    tops = lax.fori_loop(
        first_chunk, past_chunk, score_step, tuple((jnp.full((8, wide), masked_out, jnp.float32) for _ in range(3)))
    )
    row_top = [jnp.max(tops[c], axis=0, keepdims=True) for c in range(3)]
    if is_self:
        own_turned = [None] + [turned_twice(ko_ref[0, c]) for c in range(2)]
        own_score = [None] + [
            jnp.sum(q_turned[c].astype(jnp.float32) * own_turned[c], axis=0, keepdims=True)
            + own_bias_ref[0]
            for c in (1, 2)
        ]
        row_top = [row_top[0]] + [jnp.maximum(row_top[c], own_score[c]) for c in (1, 2)]
    total_ref[...] = jnp.zeros_like(total_ref)

    def value_step(chunk, sums):
        sums = list(sums)
        chunk_rows = pl.ds(pl.multiple_of(chunk * wide, wide), wide)
        values = jnp.concatenate(
            [v_ref[slot_of(place, 2 * chunk + part, blocks), 0] for part in range(2)], axis=0
        )
        for c in range(3):
            lanes = pl.ds(c * wide, wide)
            weights = jnp.exp2((score_ref[chunk_rows, lanes] - row_top[c]) * score_unit)
            sums[c] = sums[c] + fold_rows(weights, jnp.sum)
            total_ref[:, lanes] += dot_00(values, weights.astype(jnp.bfloat16))
        return tuple(sums)

    sums = lax.fori_loop(
        first_chunk, past_chunk, value_step, tuple((jnp.zeros((8, wide), jnp.float32) for _ in range(3)))
    )
    for c in range(3):
        row_sum = jnp.sum(sums[c], axis=0, keepdims=True)
        mixed = total_ref[:, c * wide : (c + 1) * wide]
        if is_self and c > 0:
            own_weight = jnp.exp2((own_score[c] - row_top[c]) * score_unit)
            row_sum = row_sum + own_weight
            value_turned = turned_twice(vo_ref[0, c - 1])
            mixed = mixed + own_weight * value_turned
        mixed = mixed / row_sum
        o_ref[0, c] = join_heads(mixed.T, half).astype(jnp.bfloat16)
        lse_ref[0, 0, :, c * wide : (c + 1) * wide] = row_top[c] * score_unit + jnp.log2(row_sum)


def backward_kernel(is_self, rows, near_tiles, *refs):
    if is_self:
        (bounds_ref, q_ref, k_ref, v_ref, o_ref, do_ref, lse_ref, ko_ref, vo_ref, bias_ref, own_bias_ref,
         dq_ref, dk_ref, dv_ref, dko_ref, dvo_ref, tiles_ref, own_sum_ref, prob_ref, grad_ref, total_ref) = refs
    else:
        (bounds_ref, q_ref, k_ref, v_ref, o_ref, do_ref, lse_ref,
         dq_ref, dk_ref, dv_ref, prob_ref, grad_ref, total_ref) = refs
    stream = pl.program_id(1)
    half = q_ref.shape[3] // 2
    wide = 2 * rows
    first_chunk = bounds_ref[stream, 0] // 2
    past_chunk = bounds_ref[stream, 1] // 2 + 1
    place, blocks = bounds_ref[stream, 2], k_ref.shape[0]
    chunk_count = blocks // 2
    q_tall = [two_heads(q_ref[0, c], half) for c in range(3)]
    do_tall = [two_heads(do_ref[0, c], half) for c in range(3)]
    q_turned = [tall.T for tall in q_tall]
    do_turned = [tall.T for tall in do_tall]
    lse = [lse_ref[0, 0, :, c * wide : (c + 1) * wide] for c in range(3)]
    centre = []
    for c in range(3):
        o_turned = turned_twice(o_ref[0, c])
        centre.append(jnp.sum(do_turned[c].astype(jnp.float32) * o_turned, axis=0, keepdims=True))
    q_all = jnp.concatenate(q_tall, axis=0)
    do_all = jnp.concatenate(do_tall, axis=0)
    total_ref[...] = jnp.zeros_like(total_ref)

    if is_self:

        @pl.when(stream == 0)
        def _():
            tiles_ref[...] = jnp.zeros_like(tiles_ref)
            own_sum_ref[...] = jnp.zeros_like(own_sum_ref)

    def blank_step(chunk, carry):
        for part in range(2):
            slot = slot_of(place, 2 * chunk + part, blocks)
            dk_ref[slot, 0] = jnp.zeros((rows, 2 * half), jnp.bfloat16)
            dv_ref[slot, 0] = jnp.zeros((rows, 2 * half), jnp.bfloat16)
        return carry

    lax.fori_loop(0, first_chunk, blank_step, 0)
    lax.fori_loop(past_chunk, chunk_count, blank_step, 0)

    def chunk_step(chunk, carry):
        for part in range(2):
            block = 2 * chunk + part
            part_rows = pl.ds(part * rows, rows)
            keys = k_ref[slot_of(place, block, blocks), 0]
            values = v_ref[slot_of(place, block, blocks), 0]
            if is_self:
                diag_tile, plain_tile = tile_of(bounds_ref, stream, block, near_tiles)
                later_tile = jnp.where(diag_tile == 0, 1, plain_tile)
                tile_index = (jnp.where(diag_tile == 0, 0, plain_tile), later_tile, later_tile)
            grad_sum = None
            for c in range(3):
                lanes = pl.ds(c * wide, wide)
                scores = dot_10(keys, q_turned[c])
                if is_self:
                    scores = scores + bias_ref[0, tile_index[c]]
                else:
                    scores = scores + shift_of(bounds_ref, stream, block)
                probs = jnp.exp2(scores * score_unit - lse[c])
                prob_ref[part_rows, lanes] = probs.astype(jnp.bfloat16)
                grads = probs * (dot_10(values, do_turned[c]) - centre[c])
                grad_ref[part_rows, lanes] = grads.astype(jnp.bfloat16)
                if is_self:
                    grad_sum = grads if grad_sum is None else grad_sum + grads
            if is_self:
                tiles_ref[0, tile_index[1]] += grad_sum
        slots = [slot_of(place, 2 * chunk + part, blocks) for part in range(2)]
        value_grads = dot_10(prob_ref[...], do_all).astype(jnp.bfloat16)
        key_grads = (0.125 * dot_10(grad_ref[...], q_all)).astype(jnp.bfloat16)
        for part in range(2):
            dv_ref[slots[part], 0] = value_grads[part * rows : (part + 1) * rows]
            dk_ref[slots[part], 0] = key_grads[part * rows : (part + 1) * rows]
        total_ref[...] += dot_00(jnp.concatenate([k_ref[slot, 0] for slot in slots], axis=0), grad_ref[...])
        return carry

    lax.fori_loop(first_chunk, past_chunk, chunk_step, 0)
    for c in range(3):
        turned = total_ref[:, c * wide : (c + 1) * wide]
        if is_self and c > 0:
            own_turned = turned_twice(ko_ref[0, c - 1])
            value_turned = turned_twice(vo_ref[0, c - 1])
            q_wide = q_turned[c].astype(jnp.float32)
            do_wide = do_turned[c].astype(jnp.float32)
            own_score = jnp.sum(q_wide * own_turned, axis=0, keepdims=True) + own_bias_ref[0]
            own_prob = jnp.exp2(own_score * score_unit - lse[c])
            own_dp = jnp.sum(do_wide * value_turned, axis=0, keepdims=True)
            own_grad = own_prob * (own_dp - centre[c])
            own_sum_ref[0] += own_grad
            own_grad = own_grad.astype(jnp.bfloat16).astype(jnp.float32)
            own_low = own_prob.astype(jnp.bfloat16).astype(jnp.float32)
            turned = turned + own_grad * own_turned
            dko = (0.125 * own_grad * q_wide).T
            dko_ref[0, c - 1] = (dko[:rows] + dko[rows:]).astype(jnp.bfloat16)
            dvo = (own_low * do_wide).T
            dvo_ref[0, c - 1] = (dvo[:rows] + dvo[rows:]).astype(jnp.bfloat16)
        dq_ref[0, c] = (0.125 * join_heads(turned.T, half)).astype(jnp.bfloat16)


def attend_forward(bounds, query, keys, values, own=None, near_tiles=0, head_size=64):
    streams, _, rows, width = query.shape
    blocks = keys.shape[0]
    length = blocks * rows
    lanes = 2 * head_size
    pairs = width // lanes
    is_self = own is not None
    row_spec = pl.BlockSpec((1, 3, rows, lanes), lambda p, n, s: (n, 0, 0, p))
    key_spec = pl.BlockSpec((blocks, 1, rows, lanes), lambda p, n, s: (0, n, 0, p))
    in_specs = [row_spec, key_spec, key_spec]
    args = [query, keys, values]
    if is_self:
        own_keys, own_values, tiles, own_bias = own
        own_spec = pl.BlockSpec((1, 2, rows, lanes), lambda p, n, s: (n, 0, 0, p))
        in_specs += [
            own_spec,
            own_spec,
            pl.BlockSpec((1,) + tiles.shape[1:], lambda p, n, s: (p, 0, 0, 0)),
            pl.BlockSpec((1, 1, 2 * rows), lambda p, n, s: (p, 0, 0)),
        ]
        args += [own_keys, own_values, tiles, own_bias]
    return pl.pallas_call(
        partial(forward_kernel, is_self, rows, near_tiles),
        grid_spec=pltpu.PrefetchScalarGridSpec(
            num_scalar_prefetch=1,
            grid=(pairs, streams),
            in_specs=in_specs,
            out_specs=[row_spec, pl.BlockSpec((1, 1, 1, 6 * rows), lambda p, n, s: (p, n, 0, 0))],
            scratch_shapes=[
                pltpu.VMEM((length, 6 * rows), jnp.float32),
                pltpu.VMEM((lanes, 6 * rows), jnp.float32),
            ],
        ),
        out_shape=[
            jax.ShapeDtypeStruct(query.shape, jnp.bfloat16),
            jax.ShapeDtypeStruct((pairs, streams, 1, 6 * rows), jnp.float32),
        ],
        compiler_params=pltpu.CompilerParams(vmem_limit_bytes=20 * 1024 * 1024),
        cost_estimate=pl.CostEstimate(flops=0, bytes_accessed=0, transcendentals=0),
    )(bounds, *args)


def attend_backward(bounds, query, keys, values, mixed, mix_grad, lse, own=None, near_tiles=0, head_size=64):
    streams, _, rows, width = query.shape
    blocks = keys.shape[0]
    length = blocks * rows
    lanes = 2 * head_size
    pairs = width // lanes
    is_self = own is not None
    row_spec = pl.BlockSpec((1, 3, rows, lanes), lambda p, n, s: (n, 0, 0, p))
    key_spec = pl.BlockSpec((blocks, 1, rows, lanes), lambda p, n, s: (0, n, 0, p))
    in_specs = [row_spec, key_spec, key_spec, row_spec, row_spec,
                pl.BlockSpec((1, 1, 1, 6 * rows), lambda p, n, s: (p, n, 0, 0))]
    args = [query, keys, values, mixed, mix_grad, lse]
    out_specs = [row_spec, key_spec, key_spec]
    out_shape = [jax.ShapeDtypeStruct(query.shape, jnp.bfloat16)] + [jax.ShapeDtypeStruct(keys.shape, jnp.bfloat16)] * 2
    if is_self:
        own_keys, own_values, tiles, own_bias = own
        own_spec = pl.BlockSpec((1, 2, rows, lanes), lambda p, n, s: (n, 0, 0, p))
        tile_spec = pl.BlockSpec((1,) + tiles.shape[1:], lambda p, n, s: (p, 0, 0, 0))
        own_bias_spec = pl.BlockSpec((1, 1, 2 * rows), lambda p, n, s: (p, 0, 0))
        in_specs += [own_spec, own_spec, tile_spec, own_bias_spec]
        args += [own_keys, own_values, tiles, own_bias]
        out_specs += [own_spec, own_spec, tile_spec, own_bias_spec]
        out_shape += [jax.ShapeDtypeStruct(own_keys.shape, jnp.bfloat16)] * 2
        out_shape += [jax.ShapeDtypeStruct(tiles.shape, jnp.float32), jax.ShapeDtypeStruct(own_bias.shape, jnp.float32)]
    return pl.pallas_call(
        partial(backward_kernel, is_self, rows, near_tiles),
        grid_spec=pltpu.PrefetchScalarGridSpec(
            num_scalar_prefetch=1,
            grid=(pairs, streams),
            in_specs=in_specs,
            out_specs=out_specs,
            scratch_shapes=[
                pltpu.VMEM((2 * rows, 6 * rows), jnp.bfloat16),
                pltpu.VMEM((2 * rows, 6 * rows), jnp.bfloat16),
                pltpu.VMEM((lanes, 6 * rows), jnp.float32),
            ],
        ),
        out_shape=out_shape,
        compiler_params=pltpu.CompilerParams(vmem_limit_bytes=20 * 1024 * 1024),
        cost_estimate=pl.CostEstimate(flops=0, bytes_accessed=0, transcendentals=0),
    )(bounds, *args)


def bucket_of(distance):
    nearby = jnp.maximum(distance, 0)
    distant = 16 + sum(((nearby >= edge).astype(jnp.int32) for edge in bucket_edges))
    return jnp.where(nearby < 16, nearby, distant)


def near_count(rows):
    gap = 1
    while rows * gap - (rows - 1) < bucket_edges[-1]:
        gap += 1
    return gap


def bias_tiles(rel_table, rows):
    heads, buckets = rel_table.shape
    near_tiles = near_count(rows)
    places = jnp.arange(rows, dtype=jnp.int32)
    distance = places[None, None, :] - places[None, :, None] + rows * jnp.arange(near_tiles, dtype=jnp.int32)[:, None, None]
    onehot = (bucket_of(distance)[..., None] == jnp.arange(buckets, dtype=jnp.int32)).astype(jnp.float32)
    shifted = 8.0 * (rel_table - rel_table[:, buckets - 1 :])
    gap = jnp.tile(places[None, :] - places[:, None], (1, 2))[None, None]
    near = jnp.concatenate(
        [
            jnp.einsum("dstk,pk->pdst", onehot, shifted[side::2], precision=lax.Precision.HIGHEST)
            for side in range(2)
        ],
        axis=-1,
    )
    diag = near[:, :1]
    tiles = jnp.concatenate(
        [
            jnp.where(gap >= 0, diag, masked_out),
            jnp.where(gap > 0, diag, masked_out),
            near[:, 1:],
            jnp.zeros_like(diag),
            jnp.full_like(diag, masked_out),
        ],
        axis=1,
    )
    own_bias = jnp.repeat(shifted[:, 0], rows).reshape(heads // 2, 1, 2 * rows)
    return tiles, own_bias, onehot


def table_grad(tile_grads, own_sums, onehot, bucket_count):
    pairs, tile_count, rows, wide = tile_grads.shape
    near_tiles = tile_count - 3
    sides = (tile_grads[..., : wide // 2], tile_grads[..., wide // 2 :])
    near_part, far_part = (
        jnp.stack(parts, axis=1)
        for parts in zip(
            *(
                (
                    jnp.einsum(
                        "pdst,dstk->pk", side[:, 1 : 1 + near_tiles], onehot, precision=lax.Precision.HIGHEST
                    ),
                    jnp.sum(side[:, 1 + near_tiles], axis=(1, 2)),
                )
                for side in sides
            )
        )
    )
    own_part = jnp.sum(own_sums.reshape(pairs, 2, wide // 2), axis=-1)
    buckets = jnp.arange(bucket_count)
    result = near_part + far_part[..., None] * (buckets == bucket_count - 1) + own_part[..., None] * (buckets == 0)
    return result.reshape(2 * pairs, bucket_count)


def norm_parts(values_in):
    centred = values_in - jnp.mean(values_in, axis=-1, keepdims=True)
    inv_scale = lax.rsqrt(jnp.mean(centred * centred, axis=-1, keepdims=True) + 1e-05)
    return (centred * inv_scale, inv_scale)


def norm_back(grad_in, normed, inv_scale, gain_row):
    scaled = grad_in * gain_row
    return inv_scale * (
        scaled
        - jnp.mean(scaled, axis=-1, keepdims=True)
        - normed * jnp.mean(scaled * normed, axis=-1, keepdims=True)
    )


def matmul(left_side, right_side):
    return jnp.einsum("...i,ij->...j", left_side, right_side, preferred_element_type=jnp.float32)


def matmul_t(left_side, right_side):
    return jnp.einsum("...j,ij->...i", left_side, right_side, preferred_element_type=jnp.float32)


def swap_core(values_in):
    size = lax.axis_size("dp")
    return lax.ppermute(values_in, "dp", [(i, i ^ 1) for i in range(size)])


def swap_chip(values_in):
    size = lax.axis_size("dp")
    return lax.ppermute(values_in, "dp", [(i, i ^ 2) for i in range(size)])


def swap_block(values_in, bit):
    size = lax.axis_size("blk")
    return lax.ppermute(values_in, "blk", [(i, i ^ bit) for i in range(size)])


def tie(value, *earlier):
    return lax.optimization_barrier((value,) + earlier)[0]


def assemble(pieces):
    count = pieces[0].shape[0]

    def ordered(at):
        def joined(*parts):
            return [jnp.concatenate([parts[at ^ index][k] for index in range(4)], axis=0) for k in range(count)]

        return joined

    return lax.switch(lax.axis_index("dp"), [ordered(at) for at in range(4)], *pieces)


def outer_low(left_side, right_side):
    return jnp.einsum("ni,nj->ij", left_side, right_side, preferred_element_type=jnp.float32)


def pick(values_in, index, axis):
    return lax.dynamic_index_in_dim(values_in, index, axis, keepdims=False)


def add_low(kept, arrived):
    return (kept.astype(jnp.float32) + arrived.astype(jnp.float32)).astype(jnp.bfloat16)


def open_core(grads):
    core = lax.axis_index("dp") % 2
    blocks = lax.axis_size("blk")

    def split(core_at):
        return jnp.stack(
            [pick(g.reshape(2, 2, blocks, g.shape[0] // (4 * blocks), g.shape[1]), core_at, 1) for g in grads], axis=2
        )

    return split(1 - core), split(core)


def open_chip(values_in):
    chip = lax.axis_index("dp") // 2
    return pick(values_in, 1 - chip, 0), pick(values_in, chip, 0)


def open_block(values_in, axis, bit):
    shape = values_in.shape
    values_in = values_in.reshape(shape[:axis] + (shape[axis] // 2, 2) + shape[axis + 1 :])
    mine = (lax.axis_index("blk") // bit) % 2
    return pick(values_in, 1 - mine, axis + 1), pick(values_in, mine, axis + 1)


def gather_far_first(values_in):
    even = [values_in]
    odd = [swap_block(values_in, 1)]
    before = values_in
    for gap in range(2, lax.axis_size("blk"), 2):
        piece = swap_block(values_in if gap <= 4 else tie(values_in, before), gap)
        before = piece
        even.append(piece)
        odd.append(swap_block(piece, 1))
    return jnp.stack(even + odd), before


def gather_near_first(values_in, *earlier):
    both = jnp.stack([values_in, swap_block(values_in, 1)])
    sent = tie(both, *earlier)
    pieces = [both] + [swap_block(sent, gap) for gap in range(2, lax.axis_size("blk"), 2)]
    return jnp.stack(pieces, axis=1).reshape((lax.axis_size("blk"),) + values_in.shape)


def fold_odd(terms):
    half = terms.shape[0] // 2
    return terms[:half], swap_block(terms[half:], 1)


def fold_even(terms):
    return sum(
        [swap_block(terms[index], 2 * index).astype(jnp.float32) for index in range(1, terms.shape[0])],
        terms[0].astype(jnp.float32),
    )


def fold_far_first(terms):
    half = terms.shape[0] // 2
    split = terms.reshape((2, half) + terms.shape[1:])
    return split[:, 0], [swap_block(split[:, index], 2 * index) for index in range(1, half)]


def sum_all(kept, come):
    return sum([piece.astype(jnp.float32) for piece in come], kept.astype(jnp.float32))


def start_exchange(values_in):
    mine = lax.axis_index("blk") // 2
    come = [swap_block(pick(values_in, mine ^ gap, 0), 2 * gap) for gap in range(1, values_in.shape[0])]
    return pick(values_in, mine, 0), come


def split_shares(share):
    share = share.astype(jnp.float32)
    return [share[k] for k in range(share.shape[0])]


def sum_everywhere(values_in):
    total = values_in + swap_core(values_in)
    total = total + swap_chip(total)
    total = total + swap_block(total, 1)
    blocks = lax.axis_size("blk")
    mine = lax.axis_index("blk") // 2
    come = jnp.stack([total] + [swap_block(total, 2 * gap) for gap in range(1, blocks // 2)])
    return sum(pick(come, mine ^ index, 0) for index in range(blocks // 2))


def shards(
    hidden,
    encoder,
    lengths,
    qkv_self,
    out_self,
    rel_table,
    qkv_cross,
    out_cross,
    ffn_in,
    ffn_out,
    norm_gain,
    norm_bias,
    cotangent,
):
    streams, _, rows, width = hidden.shape
    heads, buckets = rel_table.shape
    head_size = width // heads
    place = lax.axis_index("blk")
    main_all, main_last = gather_far_first(hidden[:, 0])
    enc_all = gather_near_first(encoder, main_last)
    low = partial(lax.convert_element_type, new_dtype=jnp.bfloat16)
    qkv_low = low(qkv_self)
    middle_low = jnp.concatenate([low(out_self)[None], low(qkv_cross), low(out_cross)[None]])
    first_low_w, second_low_w = low(ffn_in)[None], low(ffn_out)[None]
    qkv_far = swap_chip(qkv_low)
    w_qkv = assemble([qkv_low, swap_core(qkv_low), qkv_far, swap_core(qkv_far)])
    doc_ends = jnp.cumsum(lengths, axis=-1)
    begin = place * rows
    doc_begin = jnp.max(jnp.where(doc_ends <= begin, doc_ends, 0), axis=-1)
    doc_end = jnp.min(jnp.where(doc_ends > begin, doc_ends, rows * lax.axis_size("blk")), axis=-1)
    first_block = (doc_begin // rows).astype(jnp.int32)
    last_block = (doc_end // rows - 1).astype(jnp.int32)
    places = jnp.full_like(first_block, place)
    self_bounds = jnp.stack([first_block, places, places], axis=1)
    cross_bounds = jnp.stack([first_block, last_block, places], axis=1)
    near_tiles = near_count(rows)
    tiles, own_bias, onehot = bias_tiles(rel_table, rows)

    def flat(values_in):
        return values_in.reshape(-1, values_in.shape[-1])

    def tall(values_in):
        return values_in.reshape(streams, 3, rows, width)

    hidden_own = hidden[:, 1:]
    query = matmul(hidden, w_qkv[0]).astype(jnp.bfloat16)
    own_keys = matmul(hidden_own, w_qkv[1]).astype(jnp.bfloat16)
    own_values = matmul(hidden_own, w_qkv[2]).astype(jnp.bfloat16)
    middle_far = swap_chip(tie(middle_low, qkv_far))
    main_keys = matmul(main_all, w_qkv[1]).astype(jnp.bfloat16)
    main_values = matmul(main_all, w_qkv[2]).astype(jnp.bfloat16)
    own = (own_keys, own_values, tiles, own_bias)

    first_far = swap_chip(tie(first_low_w, main_values, query))
    attended, self_lse = attend_forward(
        self_bounds, query, main_keys, main_values, own, near_tiles, head_size
    )
    second_far = swap_chip(tie(second_low_w, first_far))
    middle_pieces = [middle_low, swap_core(middle_low), middle_far, swap_core(tie(middle_far, attended))]
    w_out, *c_qkv, c_out = assemble(middle_pieces)
    first_norm, first_scale = norm_parts(
        flat(hidden).astype(jnp.float32) + matmul(flat(attended), w_out)
    )
    first_out = first_norm * norm_gain[0] + norm_bias[0]
    first_low = first_out.astype(jnp.bfloat16)
    cross_query = matmul(first_low, c_qkv[0]).astype(jnp.bfloat16)
    enc_keys = matmul(enc_all, c_qkv[1]).astype(jnp.bfloat16)
    enc_values = matmul(enc_all, c_qkv[2]).astype(jnp.bfloat16)
    cross_att, cross_lse = attend_forward(
        cross_bounds, tall(cross_query), enc_keys, enc_values, None, 0, head_size
    )
    w_first, w_second = (
        assemble([shard, swap_core(shard), far, swap_core(far)])[0]
        for shard, far in ((first_low_w, tie(first_far, cross_query)), (second_low_w, tie(second_far, cross_query)))
    )
    second_norm, second_scale = norm_parts(first_out + matmul(flat(cross_att), c_out))
    second_out = second_norm * norm_gain[1] + norm_bias[1]
    second_low = second_out.astype(jnp.bfloat16)
    inner_act = matmul(second_low, w_first)
    normal_cdf = 0.5 * (1.0 + lax.erf(inner_act * math.sqrt(0.5)))
    activated = (inner_act * normal_cdf).astype(jnp.bfloat16)
    density = jnp.exp(-0.5 * inner_act * inner_act) * (1.0 / math.sqrt(2.0 * math.pi))
    act_slope = (normal_cdf + inner_act * density).astype(jnp.bfloat16)
    third_norm, third_scale = norm_parts(second_out + matmul(activated, w_second))
    output = tall((third_norm * norm_gain[2] + norm_bias[2]).astype(jnp.bfloat16))

    grad_out = flat(cotangent).astype(jnp.float32)
    gain_three = jnp.sum(grad_out * third_norm, axis=0)
    bias_three = jnp.sum(grad_out, axis=0)
    third_grad = norm_back(grad_out, third_norm, third_scale, norm_gain[2])
    third_low = third_grad.astype(jnp.bfloat16)
    second_part = outer_low(activated, third_low).astype(jnp.bfloat16)
    second_sent, second_kept = open_core([second_part])
    second_come = swap_core(second_sent)
    inner_grad = (
        matmul_t(tie(third_low, second_sent), w_second) * act_slope.astype(jnp.float32)
    ).astype(jnp.bfloat16)
    row_sent, row_kept = open_block(add_low(second_kept, second_come), 1, 1)
    row_come = swap_block(row_sent, 1)
    inner_grad = tie(inner_grad, row_sent)
    first_part = outer_low(second_low, inner_grad).astype(jnp.bfloat16)
    first_sent, first_kept = open_core([first_part])
    first_come = swap_core(first_sent)
    second_total = third_grad + matmul_t(tie(inner_grad, first_sent), w_first)
    gain_two = jnp.sum(second_total * second_norm, axis=0)
    bias_two = jnp.sum(second_total, axis=0)
    second_grad = norm_back(second_total, second_norm, second_scale, norm_gain[1])
    cross_low = second_grad.astype(jnp.bfloat16)
    first_chip_sent, first_chip_kept = open_chip(add_low(first_kept, first_come))
    first_chip_come = swap_chip(first_chip_sent)
    cross_mix_grad = tall(matmul_t(tie(cross_low, first_chip_sent), c_out).astype(jnp.bfloat16))
    cross_query_grad, enc_key_grad, enc_value_grad = attend_backward(
        cross_bounds, tall(cross_query), enc_keys, enc_values, cross_att, cross_mix_grad, cross_lse,
        None, 0, head_size,
    )
    chip_sent, chip_kept = open_chip(add_low(row_kept, tie(row_come, enc_key_grad)))
    chip_come = swap_chip(chip_sent)
    enc_key_grad = tie(enc_key_grad, chip_sent)
    encoder_terms = (matmul_t(enc_key_grad, c_qkv[1]) + matmul_t(enc_value_grad, c_qkv[2])).astype(jnp.bfloat16)
    encoder_kept, encoder_come = fold_far_first(encoder_terms)
    first_row_sent, first_row_kept = open_block(add_low(first_chip_kept, tie(first_chip_come, encoder_terms)), 0, 1)
    first_row_come = swap_block(first_row_sent, 1)
    first_total = second_grad + matmul_t(flat(tie(cross_query_grad, first_row_sent)), c_qkv[0])
    gain_one = jnp.sum(first_total * first_norm, axis=0)
    bias_one = jnp.sum(first_total, axis=0)
    first_grad = norm_back(first_total, first_norm, first_scale, norm_gain[0])
    out_low = first_grad.astype(jnp.bfloat16)
    cross_parts = [
        outer_low(flat(left), flat(right)).astype(jnp.bfloat16)
        for left, right in (
            (cross_att, cross_low),
            (first_low, cross_query_grad),
            (enc_all, tie(enc_key_grad, out_low)),
            (enc_all, enc_value_grad),
            (attended, out_low),
        )
    ]
    cross_sent, cross_kept = open_core(cross_parts)
    cross_come = swap_core(cross_sent)
    mix_grad = tall(matmul_t(tie(out_low, cross_sent), w_out).astype(jnp.bfloat16))
    cross_chip_sent, cross_chip_kept = open_chip(add_low(cross_kept, tie(cross_come, mix_grad)))
    cross_chip_come = swap_chip(cross_chip_sent)
    second_half = add_low(chip_kept, tie(chip_come, mix_grad))
    g_second = sum_all(*start_exchange(second_half))[0]
    mix_grad = tie(mix_grad, cross_chip_sent, second_half)
    query_grad, key_grad, value_grad, own_key_grad, own_value_grad, tile_grads, own_sums = attend_backward(
        self_bounds, query, main_keys, main_values, attended, mix_grad, self_lse, own, near_tiles, head_size
    )
    first_half = add_low(first_row_kept, tie(first_row_come, query_grad))
    g_first = sum_all(*start_exchange(first_half))[0]
    key_grad = tie(key_grad, first_half)
    main_terms = (matmul_t(key_grad, w_qkv[1]) + matmul_t(value_grad, w_qkv[2])).astype(jnp.bfloat16)
    main_kept, main_come = fold_odd(main_terms)
    main_come_from = main_terms
    encoder_half = sum_all(encoder_kept, [tie(piece, main_terms) for piece in encoder_come]).astype(jnp.bfloat16)
    d_encoder = sum_all(encoder_half[0], [swap_block(encoder_half[1], 1)])
    own_flat = flat(hidden_own)
    main_flat = flat(main_all)
    started = tie(query_grad, main_come_from, encoder_half)
    self_parts = [outer_low(flat(hidden), flat(started)).astype(jnp.bfloat16)] + [
        (outer_low(main_flat, flat(tie(grad, started))) + outer_low(own_flat, flat(own_grad))).astype(jnp.bfloat16)
        for grad, own_grad in ((key_grad, own_key_grad), (value_grad, own_value_grad))
    ]
    self_sent, self_kept = open_core(self_parts)
    self_come = swap_core(self_sent)
    local_grad = tall(first_grad) + matmul_t(tie(query_grad, self_sent), w_qkv[0])
    self_chip_sent, self_chip_kept = open_chip(add_low(self_kept, tie(self_come, local_grad)))
    self_chip_come = swap_chip(self_chip_sent)
    own_back = matmul_t(tie(own_key_grad, self_chip_sent), w_qkv[1]) + matmul_t(own_value_grad, w_qkv[2])
    main_half = add_low(main_kept, tie(main_come, own_back))
    main_back = fold_even(main_half)
    cross_half = add_low(cross_chip_kept, tie(cross_chip_come, main_half))
    late_sent, late_kept = open_block(
        jnp.concatenate([cross_half, add_low(self_chip_kept, tie(self_chip_come, main_half))], axis=1), 0, 1
    )
    late_half = add_low(late_kept, swap_block(late_sent, 1))
    late_share = sum_all(*start_exchange(late_half))
    g_cross_out, *g_cross, g_self_out = split_shares(late_share[:5])
    g_cross = jnp.stack(g_cross)
    g_qkv = late_share[5:]
    d_hidden = local_grad + jnp.concatenate([main_back[:, None], own_back], axis=1)
    rel_grad = table_grad(tile_grads, own_sums, onehot, buckets)
    small = jnp.concatenate(
        [
            jnp.stack([gain_one, gain_two, gain_three, bias_one, bias_two, bias_three]),
            rel_grad.reshape(-1, width) if rel_grad.size % width == 0 else
            jnp.pad(rel_grad.reshape(1, -1), ((0, 0), (0, width - rel_grad.size))),
        ]
    )
    small = sum_everywhere(small)
    return (
        output,
        d_hidden,
        d_encoder,
        g_qkv,
        g_self_out,
        small[6:].reshape(-1)[: heads * buckets].reshape(heads, buckets),
        g_cross,
        g_cross_out,
        g_first,
        g_second,
        small[0:3],
        small[3:6],
    )


def solution(mesh):
    in_specs = (
        P("dp", None, "blk", None),
        P("dp", "blk", None),
        P("dp", None),
        P(None, "dp", None),
        P("dp", None),
        P(),
        P(None, "dp", None),
        P("dp", None),
        P("dp", None),
        P("dp", None),
        P(),
        P(),
        P("dp", None, "blk", None),
    )
    out_specs = (
        P("dp", None, "blk", None),
        P("dp", None, "blk", None),
        P("dp", "blk", None),
        P(None, ("dp", "blk"), None),
        P(("dp", "blk"), None),
        P(),
        P(None, ("dp", "blk"), None),
        P(("dp", "blk"), None),
        P(("dp", "blk"), None),
        P(("dp", "blk"), None),
        P(),
        P(),
    )
    return jax.shard_map(shards, mesh=mesh, in_specs=in_specs, out_specs=out_specs, check_vma=False)
```

```python
from functools import partial
import math
import jax
import jax.numpy as jnp
from jax import lax
from jax.experimental import pallas as pl
from jax.experimental.pallas import tpu as pltpu
from jax.sharding import PartitionSpec as P

bucket_edges = tuple((math.ceil(16 * 8 ** (power / 16)) for power in range(1, 16)))
score_unit = 0.125 * math.log2(math.e)
masked_out = -1e30


def fold_rows(values_in, combine):
    return combine(values_in.reshape(values_in.shape[0] // 8, 8, values_in.shape[1]), axis=0)


def two_heads(tile, half):
    wide = tile.astype(jnp.float32)
    low_lanes = lax.broadcasted_iota(jnp.int32, wide.shape, 1) < half
    tall = jnp.concatenate([jnp.where(low_lanes, wide, 0.0), jnp.where(low_lanes, 0.0, wide)], axis=0)
    return tall.astype(jnp.bfloat16)


def turned_twice(tile):
    return jnp.concatenate([tile.astype(jnp.float32)] * 2, axis=0).T


def join_heads(tall, half):
    rows = tall.shape[0] // 2
    low_lanes = lax.broadcasted_iota(jnp.int32, (rows, tall.shape[1]), 1) < half
    return jnp.where(low_lanes, tall[:rows], tall[rows:])


def dot_00(left_side, right_side):
    return lax.dot_general(left_side, right_side, (((0,), (0,)), ((), ())), preferred_element_type=jnp.float32)


def dot_10(left_side, right_side):
    return lax.dot_general(left_side, right_side, (((1,), (0,)), ((), ())), preferred_element_type=jnp.float32)


def slot_of(place, block, blocks):
    gap = place ^ block
    return (gap >> 1) + (blocks // 2) * (gap & 1)


def tile_of(bounds_ref, stream, block, near_tiles):
    first, place = bounds_ref[stream, 0], bounds_ref[stream, 1]
    gap = place - block
    outside = (block < first) | (gap < 0)
    plain = jnp.where(outside, near_tiles + 2, jnp.minimum(gap, near_tiles) + 1)
    return jnp.where(gap == 0, 0, plain), plain


def shift_of(bounds_ref, stream, block):
    inside = (block >= bounds_ref[stream, 0]) & (block <= bounds_ref[stream, 1])
    return jnp.where(inside, 0.0, masked_out)


def forward_kernel(is_self, rows, near_tiles, *refs):
    if is_self:
        bounds_ref, q_ref, k_ref, v_ref, ko_ref, vo_ref, bias_ref, own_bias_ref, o_ref, lse_ref, score_ref, total_ref = refs
    else:
        bounds_ref, q_ref, k_ref, v_ref, o_ref, lse_ref, score_ref, total_ref = refs
    stream = pl.program_id(1)
    half = q_ref.shape[3] // 2
    wide = 2 * rows
    first_chunk = bounds_ref[stream, 0] // 2
    past_chunk = bounds_ref[stream, 1] // 2 + 1
    place, blocks = bounds_ref[stream, 2], k_ref.shape[0]
    q_turned = [two_heads(q_ref[0, c], half).T for c in range(3)]

    def score_step(chunk, tops):
        tops = list(tops)
        for part in range(2):
            block = 2 * chunk + part
            key_rows = pl.ds(pl.multiple_of(block * rows, rows), rows)
            keys = k_ref[slot_of(place, block, blocks), 0]
            if is_self:
                diag_tile, plain_tile = tile_of(bounds_ref, stream, block, near_tiles)
                later_tile = jnp.where(diag_tile == 0, 1, plain_tile)
                tile_index = (jnp.where(diag_tile == 0, 0, plain_tile), later_tile, later_tile)
            for c in range(3):
                scores = dot_10(keys, q_turned[c])
                if is_self:
                    scores = scores + bias_ref[0, tile_index[c]]
                else:
                    scores = scores + shift_of(bounds_ref, stream, block)
                score_ref[key_rows, pl.ds(c * wide, wide)] = scores
                tops[c] = jnp.maximum(tops[c], fold_rows(scores, jnp.max))
        return tuple(tops)

    tops = lax.fori_loop(
        first_chunk, past_chunk, score_step, tuple((jnp.full((8, wide), masked_out, jnp.float32) for _ in range(3)))
    )
    row_top = [jnp.max(tops[c], axis=0, keepdims=True) for c in range(3)]
    if is_self:
        own_turned = [None] + [turned_twice(ko_ref[0, c]) for c in range(2)]
        own_score = [None] + [
            jnp.sum(q_turned[c].astype(jnp.float32) * own_turned[c], axis=0, keepdims=True)
            + own_bias_ref[0]
            for c in (1, 2)
        ]
        row_top = [row_top[0]] + [jnp.maximum(row_top[c], own_score[c]) for c in (1, 2)]
    total_ref[...] = jnp.zeros_like(total_ref)

    def value_step(chunk, sums):
        sums = list(sums)
        chunk_rows = pl.ds(pl.multiple_of(chunk * wide, wide), wide)
        values = jnp.concatenate(
            [v_ref[slot_of(place, 2 * chunk + part, blocks), 0] for part in range(2)], axis=0
        )
        for c in range(3):
            lanes = pl.ds(c * wide, wide)
            weights = jnp.exp2((score_ref[chunk_rows, lanes] - row_top[c]) * score_unit)
            sums[c] = sums[c] + fold_rows(weights, jnp.sum)
            total_ref[:, lanes] += dot_00(values, weights.astype(jnp.bfloat16))
        return tuple(sums)

    sums = lax.fori_loop(
        first_chunk, past_chunk, value_step, tuple((jnp.zeros((8, wide), jnp.float32) for _ in range(3)))
    )
    for c in range(3):
        row_sum = jnp.sum(sums[c], axis=0, keepdims=True)
        mixed = total_ref[:, c * wide : (c + 1) * wide]
        if is_self and c > 0:
            own_weight = jnp.exp2((own_score[c] - row_top[c]) * score_unit)
            row_sum = row_sum + own_weight
            value_turned = turned_twice(vo_ref[0, c - 1])
            mixed = mixed + own_weight * value_turned
        mixed = mixed / row_sum
        o_ref[0, c] = join_heads(mixed.T, half).astype(jnp.bfloat16)
        lse_ref[0, 0, :, c * wide : (c + 1) * wide] = row_top[c] * score_unit + jnp.log2(row_sum)


def backward_kernel(is_self, rows, near_tiles, *refs):
    if is_self:
        (bounds_ref, q_ref, k_ref, v_ref, o_ref, do_ref, lse_ref, ko_ref, vo_ref, bias_ref, own_bias_ref,
         dq_ref, dk_ref, dv_ref, dko_ref, dvo_ref, tiles_ref, own_sum_ref, prob_ref, grad_ref, total_ref) = refs
    else:
        (bounds_ref, q_ref, k_ref, v_ref, o_ref, do_ref, lse_ref,
         dq_ref, dk_ref, dv_ref, prob_ref, grad_ref, total_ref) = refs
    stream = pl.program_id(1)
    half = q_ref.shape[3] // 2
    wide = 2 * rows
    first_chunk = bounds_ref[stream, 0] // 2
    past_chunk = bounds_ref[stream, 1] // 2 + 1
    place, blocks = bounds_ref[stream, 2], k_ref.shape[0]
    chunk_count = blocks // 2
    q_tall = [two_heads(q_ref[0, c], half) for c in range(3)]
    do_tall = [two_heads(do_ref[0, c], half) for c in range(3)]
    q_turned = [tall.T for tall in q_tall]
    do_turned = [tall.T for tall in do_tall]
    lse = [lse_ref[0, 0, :, c * wide : (c + 1) * wide] for c in range(3)]
    centre = []
    for c in range(3):
        o_turned = turned_twice(o_ref[0, c])
        centre.append(jnp.sum(do_turned[c].astype(jnp.float32) * o_turned, axis=0, keepdims=True))
    q_all = jnp.concatenate(q_tall, axis=0)
    do_all = jnp.concatenate(do_tall, axis=0)
    total_ref[...] = jnp.zeros_like(total_ref)

    if is_self:

        @pl.when(stream == 0)
        def _():
            tiles_ref[...] = jnp.zeros_like(tiles_ref)
            own_sum_ref[...] = jnp.zeros_like(own_sum_ref)

    def blank_step(chunk, carry):
        for part in range(2):
            slot = slot_of(place, 2 * chunk + part, blocks)
            dk_ref[slot, 0] = jnp.zeros((rows, 2 * half), jnp.bfloat16)
            dv_ref[slot, 0] = jnp.zeros((rows, 2 * half), jnp.bfloat16)
        return carry

    lax.fori_loop(0, first_chunk, blank_step, 0)
    lax.fori_loop(past_chunk, chunk_count, blank_step, 0)

    def chunk_step(chunk, carry):
        for part in range(2):
            block = 2 * chunk + part
            part_rows = pl.ds(part * rows, rows)
            keys = k_ref[slot_of(place, block, blocks), 0]
            values = v_ref[slot_of(place, block, blocks), 0]
            if is_self:
                diag_tile, plain_tile = tile_of(bounds_ref, stream, block, near_tiles)
                later_tile = jnp.where(diag_tile == 0, 1, plain_tile)
                tile_index = (jnp.where(diag_tile == 0, 0, plain_tile), later_tile, later_tile)
            grad_sum = None
            for c in range(3):
                lanes = pl.ds(c * wide, wide)
                scores = dot_10(keys, q_turned[c])
                if is_self:
                    scores = scores + bias_ref[0, tile_index[c]]
                else:
                    scores = scores + shift_of(bounds_ref, stream, block)
                probs = jnp.exp2(scores * score_unit - lse[c])
                prob_ref[part_rows, lanes] = probs.astype(jnp.bfloat16)
                grads = probs * (dot_10(values, do_turned[c]) - centre[c])
                grad_ref[part_rows, lanes] = grads.astype(jnp.bfloat16)
                if is_self:
                    grad_sum = grads if grad_sum is None else grad_sum + grads
            if is_self:
                tiles_ref[0, tile_index[1]] += grad_sum
        slots = [slot_of(place, 2 * chunk + part, blocks) for part in range(2)]
        value_grads = dot_10(prob_ref[...], do_all).astype(jnp.bfloat16)
        key_grads = (0.125 * dot_10(grad_ref[...], q_all)).astype(jnp.bfloat16)
        for part in range(2):
            dv_ref[slots[part], 0] = value_grads[part * rows : (part + 1) * rows]
            dk_ref[slots[part], 0] = key_grads[part * rows : (part + 1) * rows]
        total_ref[...] += dot_00(jnp.concatenate([k_ref[slot, 0] for slot in slots], axis=0), grad_ref[...])
        return carry

    lax.fori_loop(first_chunk, past_chunk, chunk_step, 0)
    for c in range(3):
        turned = total_ref[:, c * wide : (c + 1) * wide]
        if is_self and c > 0:
            own_turned = turned_twice(ko_ref[0, c - 1])
            value_turned = turned_twice(vo_ref[0, c - 1])
            q_wide = q_turned[c].astype(jnp.float32)
            do_wide = do_turned[c].astype(jnp.float32)
            own_score = jnp.sum(q_wide * own_turned, axis=0, keepdims=True) + own_bias_ref[0]
            own_prob = jnp.exp2(own_score * score_unit - lse[c])
            own_dp = jnp.sum(do_wide * value_turned, axis=0, keepdims=True)
            own_grad = own_prob * (own_dp - centre[c])
            own_sum_ref[0] += own_grad
            own_grad = own_grad.astype(jnp.bfloat16).astype(jnp.float32)
            own_low = own_prob.astype(jnp.bfloat16).astype(jnp.float32)
            turned = turned + own_grad * own_turned
            dko = (0.125 * own_grad * q_wide).T
            dko_ref[0, c - 1] = (dko[:rows] + dko[rows:]).astype(jnp.bfloat16)
            dvo = (own_low * do_wide).T
            dvo_ref[0, c - 1] = (dvo[:rows] + dvo[rows:]).astype(jnp.bfloat16)
        dq_ref[0, c] = (0.125 * join_heads(turned.T, half)).astype(jnp.bfloat16)


def attend_forward(bounds, query, keys, values, own=None, near_tiles=0, head_size=64):
    streams, _, rows, width = query.shape
    blocks = keys.shape[0]
    length = blocks * rows
    lanes = 2 * head_size
    pairs = width // lanes
    is_self = own is not None
    row_spec = pl.BlockSpec((1, 3, rows, lanes), lambda p, n, s: (n, 0, 0, p))
    key_spec = pl.BlockSpec((blocks, 1, rows, lanes), lambda p, n, s: (0, n, 0, p))
    in_specs = [row_spec, key_spec, key_spec]
    args = [query, keys, values]
    if is_self:
        own_keys, own_values, tiles, own_bias = own
        own_spec = pl.BlockSpec((1, 2, rows, lanes), lambda p, n, s: (n, 0, 0, p))
        in_specs += [
            own_spec,
            own_spec,
            pl.BlockSpec((1,) + tiles.shape[1:], lambda p, n, s: (p, 0, 0, 0)),
            pl.BlockSpec((1, 1, 2 * rows), lambda p, n, s: (p, 0, 0)),
        ]
        args += [own_keys, own_values, tiles, own_bias]
    return pl.pallas_call(
        partial(forward_kernel, is_self, rows, near_tiles),
        grid_spec=pltpu.PrefetchScalarGridSpec(
            num_scalar_prefetch=1,
            grid=(pairs, streams),
            in_specs=in_specs,
            out_specs=[row_spec, pl.BlockSpec((1, 1, 1, 6 * rows), lambda p, n, s: (p, n, 0, 0))],
            scratch_shapes=[
                pltpu.VMEM((length, 6 * rows), jnp.float32),
                pltpu.VMEM((lanes, 6 * rows), jnp.float32),
            ],
        ),
        out_shape=[
            jax.ShapeDtypeStruct(query.shape, jnp.bfloat16),
            jax.ShapeDtypeStruct((pairs, streams, 1, 6 * rows), jnp.float32),
        ],
        compiler_params=pltpu.CompilerParams(vmem_limit_bytes=20 * 1024 * 1024),
        cost_estimate=pl.CostEstimate(flops=0, bytes_accessed=0, transcendentals=0),
    )(bounds, *args)


def attend_backward(bounds, query, keys, values, mixed, mix_grad, lse, own=None, near_tiles=0, head_size=64):
    streams, _, rows, width = query.shape
    blocks = keys.shape[0]
    length = blocks * rows
    lanes = 2 * head_size
    pairs = width // lanes
    is_self = own is not None
    row_spec = pl.BlockSpec((1, 3, rows, lanes), lambda p, n, s: (n, 0, 0, p))
    key_spec = pl.BlockSpec((blocks, 1, rows, lanes), lambda p, n, s: (0, n, 0, p))
    in_specs = [row_spec, key_spec, key_spec, row_spec, row_spec,
                pl.BlockSpec((1, 1, 1, 6 * rows), lambda p, n, s: (p, n, 0, 0))]
    args = [query, keys, values, mixed, mix_grad, lse]
    out_specs = [row_spec, key_spec, key_spec]
    out_shape = [jax.ShapeDtypeStruct(query.shape, jnp.bfloat16)] + [jax.ShapeDtypeStruct(keys.shape, jnp.bfloat16)] * 2
    if is_self:
        own_keys, own_values, tiles, own_bias = own
        own_spec = pl.BlockSpec((1, 2, rows, lanes), lambda p, n, s: (n, 0, 0, p))
        tile_spec = pl.BlockSpec((1,) + tiles.shape[1:], lambda p, n, s: (p, 0, 0, 0))
        own_bias_spec = pl.BlockSpec((1, 1, 2 * rows), lambda p, n, s: (p, 0, 0))
        in_specs += [own_spec, own_spec, tile_spec, own_bias_spec]
        args += [own_keys, own_values, tiles, own_bias]
        out_specs += [own_spec, own_spec, tile_spec, own_bias_spec]
        out_shape += [jax.ShapeDtypeStruct(own_keys.shape, jnp.bfloat16)] * 2
        out_shape += [jax.ShapeDtypeStruct(tiles.shape, jnp.float32), jax.ShapeDtypeStruct(own_bias.shape, jnp.float32)]
    return pl.pallas_call(
        partial(backward_kernel, is_self, rows, near_tiles),
        grid_spec=pltpu.PrefetchScalarGridSpec(
            num_scalar_prefetch=1,
            grid=(pairs, streams),
            in_specs=in_specs,
            out_specs=out_specs,
            scratch_shapes=[
                pltpu.VMEM((2 * rows, 6 * rows), jnp.bfloat16),
                pltpu.VMEM((2 * rows, 6 * rows), jnp.bfloat16),
                pltpu.VMEM((lanes, 6 * rows), jnp.float32),
            ],
        ),
        out_shape=out_shape,
        compiler_params=pltpu.CompilerParams(vmem_limit_bytes=20 * 1024 * 1024),
        cost_estimate=pl.CostEstimate(flops=0, bytes_accessed=0, transcendentals=0),
    )(bounds, *args)


def bucket_of(distance):
    nearby = jnp.maximum(distance, 0)
    distant = 16 + sum(((nearby >= edge).astype(jnp.int32) for edge in bucket_edges))
    return jnp.where(nearby < 16, nearby, distant)


def near_count(rows):
    gap = 1
    while rows * gap - (rows - 1) < bucket_edges[-1]:
        gap += 1
    return gap


def bias_tiles(rel_table, rows):
    heads, buckets = rel_table.shape
    near_tiles = near_count(rows)
    places = jnp.arange(rows, dtype=jnp.int32)
    distance = places[None, None, :] - places[None, :, None] + rows * jnp.arange(near_tiles, dtype=jnp.int32)[:, None, None]
    onehot = (bucket_of(distance)[..., None] == jnp.arange(buckets, dtype=jnp.int32)).astype(jnp.float32)
    shifted = 8.0 * (rel_table - rel_table[:, buckets - 1 :])
    gap = jnp.tile(places[None, :] - places[:, None], (1, 2))[None, None]
    near = jnp.concatenate(
        [
            jnp.einsum("dstk,pk->pdst", onehot, shifted[side::2], precision=lax.Precision.HIGHEST)
            for side in range(2)
        ],
        axis=-1,
    )
    diag = near[:, :1]
    tiles = jnp.concatenate(
        [
            jnp.where(gap >= 0, diag, masked_out),
            jnp.where(gap > 0, diag, masked_out),
            near[:, 1:],
            jnp.zeros_like(diag),
            jnp.full_like(diag, masked_out),
        ],
        axis=1,
    )
    own_bias = jnp.repeat(shifted[:, 0], rows).reshape(heads // 2, 1, 2 * rows)
    return tiles, own_bias, onehot


def table_grad(tile_grads, own_sums, onehot, bucket_count):
    pairs, tile_count, rows, wide = tile_grads.shape
    near_tiles = tile_count - 3
    sides = (tile_grads[..., : wide // 2], tile_grads[..., wide // 2 :])
    near_part, far_part = (
        jnp.stack(parts, axis=1)
        for parts in zip(
            *(
                (
                    jnp.einsum(
                        "pdst,dstk->pk", side[:, 1 : 1 + near_tiles], onehot, precision=lax.Precision.HIGHEST
                    ),
                    jnp.sum(side[:, 1 + near_tiles], axis=(1, 2)),
                )
                for side in sides
            )
        )
    )
    own_part = jnp.sum(own_sums.reshape(pairs, 2, wide // 2), axis=-1)
    buckets = jnp.arange(bucket_count)
    result = near_part + far_part[..., None] * (buckets == bucket_count - 1) + own_part[..., None] * (buckets == 0)
    return result.reshape(2 * pairs, bucket_count)


def norm_parts(values_in):
    centred = values_in - jnp.mean(values_in, axis=-1, keepdims=True)
    inv_scale = lax.rsqrt(jnp.mean(centred * centred, axis=-1, keepdims=True) + 1e-05)
    return (centred * inv_scale, inv_scale)


def norm_back(grad_in, normed, inv_scale, gain_row):
    scaled = grad_in * gain_row
    return inv_scale * (
        scaled
        - jnp.mean(scaled, axis=-1, keepdims=True)
        - normed * jnp.mean(scaled * normed, axis=-1, keepdims=True)
    )


def matmul(left_side, right_side):
    return jnp.einsum("...i,ij->...j", left_side, right_side, preferred_element_type=jnp.float32)


def matmul_t(left_side, right_side):
    return jnp.einsum("...j,ij->...i", left_side, right_side, preferred_element_type=jnp.float32)


def swap_core(values_in):
    size = lax.axis_size("dp")
    return lax.ppermute(values_in, "dp", [(i, i ^ 1) for i in range(size)])


def swap_chip(values_in):
    size = lax.axis_size("dp")
    return lax.ppermute(values_in, "dp", [(i, i ^ 2) for i in range(size)])


def swap_block(values_in, bit):
    size = lax.axis_size("blk")
    return lax.ppermute(values_in, "blk", [(i, i ^ bit) for i in range(size)])


def tie(value, *earlier):
    return lax.optimization_barrier((value,) + earlier)[0]


def assemble(pieces):
    count = pieces[0].shape[0]

    def ordered(at):
        def joined(*parts):
            return [jnp.concatenate([parts[at ^ index][k] for index in range(4)], axis=0) for k in range(count)]

        return joined

    return lax.switch(lax.axis_index("dp"), [ordered(at) for at in range(4)], *pieces)


def outer_low(left_side, right_side):
    return jnp.einsum("ni,nj->ij", left_side, right_side, preferred_element_type=jnp.float32)


def pick(values_in, index, axis):
    return lax.dynamic_index_in_dim(values_in, index, axis, keepdims=False)


def add_low(kept, arrived):
    return (kept.astype(jnp.float32) + arrived.astype(jnp.float32)).astype(jnp.bfloat16)


def open_core(grads):
    core = lax.axis_index("dp") % 2
    blocks = lax.axis_size("blk")

    def split(core_at):
        return jnp.stack(
            [pick(g.reshape(2, 2, blocks, g.shape[0] // (4 * blocks), g.shape[1]), core_at, 1) for g in grads], axis=2
        )

    return split(1 - core), split(core)


def open_chip(values_in):
    chip = lax.axis_index("dp") // 2
    return pick(values_in, 1 - chip, 0), pick(values_in, chip, 0)


def open_block(values_in, axis, bit):
    shape = values_in.shape
    values_in = values_in.reshape(shape[:axis] + (shape[axis] // 2, 2) + shape[axis + 1 :])
    mine = (lax.axis_index("blk") // bit) % 2
    return pick(values_in, 1 - mine, axis + 1), pick(values_in, mine, axis + 1)


def gather_far_first(values_in):
    even = [values_in]
    odd = [swap_block(values_in, 1)]
    before = values_in
    for gap in range(2, lax.axis_size("blk"), 2):
        piece = swap_block(values_in if gap <= 4 else tie(values_in, before), gap)
        before = piece
        even.append(piece)
        odd.append(swap_block(piece, 1))
    return jnp.stack(even + odd), before


def gather_near_first(values_in, *earlier):
    both = jnp.stack([values_in, swap_block(values_in, 1)])
    sent = tie(both, *earlier)
    pieces = [both] + [swap_block(sent, gap) for gap in range(2, lax.axis_size("blk"), 2)]
    return jnp.stack(pieces, axis=1).reshape((lax.axis_size("blk"),) + values_in.shape)


def fold_odd(terms):
    half = terms.shape[0] // 2
    return terms[:half], swap_block(terms[half:], 1)


def fold_even(terms):
    return sum(
        [swap_block(terms[index], 2 * index).astype(jnp.float32) for index in range(1, terms.shape[0])],
        terms[0].astype(jnp.float32),
    )


def fold_far_first(terms):
    half = terms.shape[0] // 2
    split = terms.reshape((2, half) + terms.shape[1:])
    return split[:, 0], [swap_block(split[:, index], 2 * index) for index in range(1, half)]


def sum_all(kept, come):
    return sum([piece.astype(jnp.float32) for piece in come], kept.astype(jnp.float32))


def start_exchange(values_in):
    mine = lax.axis_index("blk") // 2
    come = [swap_block(pick(values_in, mine ^ gap, 0), 2 * gap) for gap in range(1, values_in.shape[0])]
    return pick(values_in, mine, 0), come


def split_shares(share):
    share = share.astype(jnp.float32)
    return [share[k] for k in range(share.shape[0])]


def sum_everywhere(values_in):
    blocks = lax.axis_size("blk")
    mine = lax.axis_index("blk") // 2
    come = jnp.stack([values_in] + [swap_block(values_in, 2 * gap) for gap in range(1, blocks // 2)])
    total = sum(pick(come, mine ^ index, 0) for index in range(blocks // 2))
    total = total + swap_core(total)
    total = total + swap_block(total, 1)
    return total + swap_chip(total)


def shards(
    hidden,
    encoder,
    lengths,
    qkv_self,
    out_self,
    rel_table,
    qkv_cross,
    out_cross,
    ffn_in,
    ffn_out,
    norm_gain,
    norm_bias,
    cotangent,
):
    streams, _, rows, width = hidden.shape
    heads, buckets = rel_table.shape
    head_size = width // heads
    place = lax.axis_index("blk")
    main_all, main_last = gather_far_first(hidden[:, 0])
    enc_all = gather_near_first(encoder, main_last)
    low = partial(lax.convert_element_type, new_dtype=jnp.bfloat16)
    qkv_low = low(qkv_self)
    middle_low = jnp.concatenate([low(out_self)[None], low(qkv_cross), low(out_cross)[None]])
    first_low_w, second_low_w = low(ffn_in)[None], low(ffn_out)[None]
    qkv_far = swap_chip(qkv_low)
    w_qkv = assemble([qkv_low, swap_core(qkv_low), qkv_far, swap_core(qkv_far)])
    doc_ends = jnp.cumsum(lengths, axis=-1)
    begin = place * rows
    doc_begin = jnp.max(jnp.where(doc_ends <= begin, doc_ends, 0), axis=-1)
    doc_end = jnp.min(jnp.where(doc_ends > begin, doc_ends, rows * lax.axis_size("blk")), axis=-1)
    first_block = (doc_begin // rows).astype(jnp.int32)
    last_block = (doc_end // rows - 1).astype(jnp.int32)
    places = jnp.full_like(first_block, place)
    self_bounds = jnp.stack([first_block, places, places], axis=1)
    cross_bounds = jnp.stack([first_block, last_block, places], axis=1)
    near_tiles = near_count(rows)
    tiles, own_bias, onehot = bias_tiles(rel_table, rows)

    def flat(values_in):
        return values_in.reshape(-1, values_in.shape[-1])

    def tall(values_in):
        return values_in.reshape(streams, 3, rows, width)

    hidden_own = hidden[:, 1:]
    query = matmul(hidden, w_qkv[0]).astype(jnp.bfloat16)
    own_keys = matmul(hidden_own, w_qkv[1]).astype(jnp.bfloat16)
    own_values = matmul(hidden_own, w_qkv[2]).astype(jnp.bfloat16)
    middle_far = swap_chip(tie(middle_low, qkv_far))
    main_keys = matmul(main_all, w_qkv[1]).astype(jnp.bfloat16)
    main_values = matmul(main_all, w_qkv[2]).astype(jnp.bfloat16)
    own = (own_keys, own_values, tiles, own_bias)

    first_far = swap_chip(tie(first_low_w, main_values, query))
    attended, self_lse = attend_forward(
        self_bounds, query, main_keys, main_values, own, near_tiles, head_size
    )
    second_far = swap_chip(tie(second_low_w, first_far))
    middle_pieces = [middle_low, swap_core(middle_low), middle_far, swap_core(tie(middle_far, attended))]
    w_out, *c_qkv, c_out = assemble(middle_pieces)
    first_norm, first_scale = norm_parts(
        flat(hidden).astype(jnp.float32) + matmul(flat(attended), w_out)
    )
    first_out = first_norm * norm_gain[0] + norm_bias[0]
    first_low = first_out.astype(jnp.bfloat16)
    cross_query = matmul(first_low, c_qkv[0]).astype(jnp.bfloat16)
    enc_keys = matmul(enc_all, c_qkv[1]).astype(jnp.bfloat16)
    enc_values = matmul(enc_all, c_qkv[2]).astype(jnp.bfloat16)
    cross_att, cross_lse = attend_forward(
        cross_bounds, tall(cross_query), enc_keys, enc_values, None, 0, head_size
    )
    w_first, w_second = (
        assemble([shard, swap_core(shard), far, swap_core(far)])[0]
        for shard, far in ((first_low_w, tie(first_far, cross_query)), (second_low_w, tie(second_far, cross_query)))
    )
    second_norm, second_scale = norm_parts(first_out + matmul(flat(cross_att), c_out))
    second_out = second_norm * norm_gain[1] + norm_bias[1]
    second_low = second_out.astype(jnp.bfloat16)
    inner_act = matmul(second_low, w_first)
    normal_cdf = 0.5 * (1.0 + lax.erf(inner_act * math.sqrt(0.5)))
    activated = (inner_act * normal_cdf).astype(jnp.bfloat16)
    density = jnp.exp(-0.5 * inner_act * inner_act) * (1.0 / math.sqrt(2.0 * math.pi))
    act_slope = (normal_cdf + inner_act * density).astype(jnp.bfloat16)
    third_norm, third_scale = norm_parts(second_out + matmul(activated, w_second))
    output = tall((third_norm * norm_gain[2] + norm_bias[2]).astype(jnp.bfloat16))

    grad_out = flat(cotangent).astype(jnp.float32)
    gain_three = jnp.sum(grad_out * third_norm, axis=0)
    bias_three = jnp.sum(grad_out, axis=0)
    third_grad = norm_back(grad_out, third_norm, third_scale, norm_gain[2])
    third_low = third_grad.astype(jnp.bfloat16)
    second_part = outer_low(activated, third_low).astype(jnp.bfloat16)
    second_sent, second_kept = open_core([second_part])
    second_come = swap_core(second_sent)
    inner_grad = (
        matmul_t(tie(third_low, second_sent), w_second) * act_slope.astype(jnp.float32)
    ).astype(jnp.bfloat16)
    row_sent, row_kept = open_block(add_low(second_kept, second_come), 1, 1)
    row_come = swap_block(row_sent, 1)
    inner_grad = tie(inner_grad, row_sent)
    first_part = outer_low(second_low, inner_grad).astype(jnp.bfloat16)
    first_sent, first_kept = open_core([first_part])
    first_come = swap_core(first_sent)
    second_total = third_grad + matmul_t(tie(inner_grad, first_sent), w_first)
    gain_two = jnp.sum(second_total * second_norm, axis=0)
    bias_two = jnp.sum(second_total, axis=0)
    second_grad = norm_back(second_total, second_norm, second_scale, norm_gain[1])
    cross_low = second_grad.astype(jnp.bfloat16)
    first_chip_sent, first_chip_kept = open_chip(add_low(first_kept, first_come))
    first_chip_come = swap_chip(first_chip_sent)
    cross_mix_grad = tall(matmul_t(tie(cross_low, first_chip_sent), c_out).astype(jnp.bfloat16))
    cross_query_grad, enc_key_grad, enc_value_grad = attend_backward(
        cross_bounds, tall(cross_query), enc_keys, enc_values, cross_att, cross_mix_grad, cross_lse,
        None, 0, head_size,
    )
    chip_sent, chip_kept = open_chip(add_low(row_kept, tie(row_come, enc_key_grad)))
    chip_come = swap_chip(chip_sent)
    enc_key_grad = tie(enc_key_grad, chip_sent)
    encoder_terms = (matmul_t(enc_key_grad, c_qkv[1]) + matmul_t(enc_value_grad, c_qkv[2])).astype(jnp.bfloat16)
    encoder_kept, encoder_come = fold_far_first(encoder_terms)
    first_row_sent, first_row_kept = open_block(add_low(first_chip_kept, tie(first_chip_come, encoder_terms)), 0, 1)
    first_row_come = swap_block(first_row_sent, 1)
    first_total = second_grad + matmul_t(flat(tie(cross_query_grad, first_row_sent)), c_qkv[0])
    gain_one = jnp.sum(first_total * first_norm, axis=0)
    bias_one = jnp.sum(first_total, axis=0)
    first_grad = norm_back(first_total, first_norm, first_scale, norm_gain[0])
    out_low = first_grad.astype(jnp.bfloat16)
    cross_parts = [
        outer_low(flat(left), flat(right)).astype(jnp.bfloat16)
        for left, right in (
            (cross_att, cross_low),
            (first_low, cross_query_grad),
            (enc_all, tie(enc_key_grad, out_low)),
            (enc_all, enc_value_grad),
            (attended, out_low),
        )
    ]
    cross_sent, cross_kept = open_core(cross_parts)
    cross_come = swap_core(cross_sent)
    mix_grad = tall(matmul_t(tie(out_low, cross_sent), w_out).astype(jnp.bfloat16))
    cross_chip_sent, cross_chip_kept = open_chip(add_low(cross_kept, tie(cross_come, mix_grad)))
    cross_chip_come = swap_chip(cross_chip_sent)
    second_half = add_low(chip_kept, tie(chip_come, mix_grad))
    mix_grad = tie(mix_grad, cross_chip_sent, second_half)
    query_grad, key_grad, value_grad, own_key_grad, own_value_grad, tile_grads, own_sums = attend_backward(
        self_bounds, query, main_keys, main_values, attended, mix_grad, self_lse, own, near_tiles, head_size
    )
    first_half = add_low(first_row_kept, tie(first_row_come, query_grad))
    main_terms = (matmul_t(key_grad, w_qkv[1]) + matmul_t(value_grad, w_qkv[2])).astype(jnp.bfloat16)
    main_kept, main_come = fold_odd(main_terms)
    main_come_from = main_terms
    encoder_half = sum_all(encoder_kept, [tie(piece, main_terms) for piece in encoder_come]).astype(jnp.bfloat16)
    d_encoder = sum_all(encoder_half[0], [swap_block(encoder_half[1], 1)])
    own_flat = flat(hidden_own)
    main_flat = flat(main_all)
    started = tie(query_grad, main_come_from, encoder_half)
    self_parts = [outer_low(flat(hidden), flat(started)).astype(jnp.bfloat16)] + [
        (outer_low(main_flat, flat(tie(grad, started))) + outer_low(own_flat, flat(own_grad))).astype(jnp.bfloat16)
        for grad, own_grad in ((key_grad, own_key_grad), (value_grad, own_value_grad))
    ]
    self_sent, self_kept = open_core(self_parts)
    self_come = swap_core(self_sent)
    main_half = add_low(main_kept, tie(main_come, self_sent))
    main_back = fold_even(main_half)
    ffn_half = jnp.concatenate(
        [half.reshape(half.shape[0], -1, width) for half in (second_half, tie(first_half, main_half))], axis=1
    )
    ffn_share = sum_all(*start_exchange(ffn_half))
    g_second = ffn_share[: second_part.shape[0] // (4 * lax.axis_size("blk"))]
    g_first = ffn_share[g_second.shape[0] :].reshape(-1, first_part.shape[1])
    local_grad = tall(first_grad) + matmul_t(tie(query_grad, self_sent), w_qkv[0])
    self_chip_sent, self_chip_kept = open_chip(add_low(self_kept, tie(self_come, local_grad)))
    self_chip_come = swap_chip(self_chip_sent)
    own_back = matmul_t(tie(own_key_grad, self_chip_sent), w_qkv[1]) + matmul_t(own_value_grad, w_qkv[2])
    cross_half = add_low(cross_chip_kept, tie(cross_chip_come, main_half))
    late_sent, late_kept = open_block(
        jnp.concatenate([cross_half, add_low(self_chip_kept, tie(self_chip_come, main_half))], axis=1), 0, 1
    )
    late_half = add_low(late_kept, swap_block(late_sent, 1))
    late_share = sum_all(*start_exchange(late_half))
    g_cross_out, *g_cross, g_self_out = split_shares(late_share[:5])
    g_cross = jnp.stack(g_cross)
    g_qkv = late_share[5:]
    d_hidden = local_grad + jnp.concatenate([main_back[:, None], own_back], axis=1)
    rel_grad = table_grad(tile_grads, own_sums, onehot, buckets)
    small = jnp.concatenate(
        [
            jnp.stack([gain_one, gain_two, gain_three, bias_one, bias_two, bias_three]),
            rel_grad.reshape(-1, width) if rel_grad.size % width == 0 else
            jnp.pad(rel_grad.reshape(1, -1), ((0, 0), (0, width - rel_grad.size))),
        ]
    )
    small = sum_everywhere(small)
    return (
        output,
        d_hidden,
        d_encoder,
        g_qkv,
        g_self_out,
        small[6:].reshape(-1)[: heads * buckets].reshape(heads, buckets),
        g_cross,
        g_cross_out,
        g_first,
        g_second,
        small[0:3],
        small[3:6],
    )


def solution(mesh):
    in_specs = (
        P("dp", None, "blk", None),
        P("dp", "blk", None),
        P("dp", None),
        P(None, "dp", None),
        P("dp", None),
        P(),
        P(None, "dp", None),
        P("dp", None),
        P("dp", None),
        P("dp", None),
        P(),
        P(),
        P("dp", None, "blk", None),
    )
    out_specs = (
        P("dp", None, "blk", None),
        P("dp", None, "blk", None),
        P("dp", "blk", None),
        P(None, ("dp", "blk"), None),
        P(("dp", "blk"), None),
        P(),
        P(None, ("dp", "blk"), None),
        P(("dp", "blk"), None),
        P(("dp", "blk"), None),
        P(("dp", "blk"), None),
        P(),
        P(),
    )
    return jax.shard_map(shards, mesh=mesh, in_specs=in_specs, out_specs=out_specs, check_vma=False)
```

```python
from functools import partial
import math
import jax
import jax.numpy as jnp
from jax import lax
from jax.experimental import pallas as pl
from jax.experimental.pallas import tpu as pltpu
from jax.sharding import PartitionSpec as P

bucket_edges = tuple((math.ceil(16 * 8 ** (power / 16)) for power in range(1, 16)))
score_unit = 0.125 * math.log2(math.e)
masked_out = -1e30


def fold_rows(values_in, combine):
    return combine(values_in.reshape(values_in.shape[0] // 8, 8, values_in.shape[1]), axis=0)


def two_heads(tile, half):
    wide = tile.astype(jnp.float32)
    low_lanes = lax.broadcasted_iota(jnp.int32, wide.shape, 1) < half
    tall = jnp.concatenate([jnp.where(low_lanes, wide, 0.0), jnp.where(low_lanes, 0.0, wide)], axis=0)
    return tall.astype(jnp.bfloat16)


def turned_twice(tile):
    return jnp.concatenate([tile.astype(jnp.float32)] * 2, axis=0).T


def join_heads(tall, half):
    rows = tall.shape[0] // 2
    low_lanes = lax.broadcasted_iota(jnp.int32, (rows, tall.shape[1]), 1) < half
    return jnp.where(low_lanes, tall[:rows], tall[rows:])


def dot_00(left_side, right_side):
    return lax.dot_general(left_side, right_side, (((0,), (0,)), ((), ())), preferred_element_type=jnp.float32)


def dot_10(left_side, right_side):
    return lax.dot_general(left_side, right_side, (((1,), (0,)), ((), ())), preferred_element_type=jnp.float32)


def slot_of(place, block, blocks):
    gap = place ^ block
    return (gap >> 1) + (blocks // 2) * (gap & 1)


def tile_of(bounds_ref, stream, block, near_tiles):
    first, place = bounds_ref[stream, 0], bounds_ref[stream, 1]
    gap = place - block
    outside = (block < first) | (gap < 0)
    plain = jnp.where(outside, near_tiles + 2, jnp.minimum(gap, near_tiles) + 1)
    return jnp.where(gap == 0, 0, plain), plain


def shift_of(bounds_ref, stream, block):
    inside = (block >= bounds_ref[stream, 0]) & (block <= bounds_ref[stream, 1])
    return jnp.where(inside, 0.0, masked_out)


def forward_kernel(is_self, rows, near_tiles, *refs):
    if is_self:
        bounds_ref, q_ref, k_ref, v_ref, ko_ref, vo_ref, bias_ref, own_bias_ref, o_ref, lse_ref, score_ref, total_ref = refs
    else:
        bounds_ref, q_ref, k_ref, v_ref, o_ref, lse_ref, score_ref, total_ref = refs
    stream = pl.program_id(1)
    half = q_ref.shape[3] // 2
    wide = 2 * rows
    first_chunk = bounds_ref[stream, 0] // 2
    past_chunk = bounds_ref[stream, 1] // 2 + 1
    place, blocks = bounds_ref[stream, 2], k_ref.shape[0]
    q_turned = [two_heads(q_ref[0, c], half).T for c in range(3)]

    def score_step(chunk, tops):
        tops = list(tops)
        for part in range(2):
            block = 2 * chunk + part
            key_rows = pl.ds(pl.multiple_of(block * rows, rows), rows)
            keys = k_ref[slot_of(place, block, blocks), 0]
            if is_self:
                diag_tile, plain_tile = tile_of(bounds_ref, stream, block, near_tiles)
                later_tile = jnp.where(diag_tile == 0, 1, plain_tile)
                tile_index = (jnp.where(diag_tile == 0, 0, plain_tile), later_tile, later_tile)
            for c in range(3):
                scores = dot_10(keys, q_turned[c])
                if is_self:
                    scores = scores + bias_ref[0, tile_index[c]]
                else:
                    scores = scores + shift_of(bounds_ref, stream, block)
                score_ref[key_rows, pl.ds(c * wide, wide)] = scores
                tops[c] = jnp.maximum(tops[c], fold_rows(scores, jnp.max))
        return tuple(tops)

    tops = lax.fori_loop(
        first_chunk, past_chunk, score_step, tuple((jnp.full((8, wide), masked_out, jnp.float32) for _ in range(3)))
    )
    row_top = [jnp.max(tops[c], axis=0, keepdims=True) for c in range(3)]
    if is_self:
        own_turned = [None] + [turned_twice(ko_ref[0, c]) for c in range(2)]
        own_score = [None] + [
            jnp.sum(q_turned[c].astype(jnp.float32) * own_turned[c], axis=0, keepdims=True)
            + own_bias_ref[0]
            for c in (1, 2)
        ]
        row_top = [row_top[0]] + [jnp.maximum(row_top[c], own_score[c]) for c in (1, 2)]
    total_ref[...] = jnp.zeros_like(total_ref)

    def value_step(chunk, sums):
        sums = list(sums)
        chunk_rows = pl.ds(pl.multiple_of(chunk * wide, wide), wide)
        values = jnp.concatenate(
            [v_ref[slot_of(place, 2 * chunk + part, blocks), 0] for part in range(2)], axis=0
        )
        for c in range(3):
            lanes = pl.ds(c * wide, wide)
            weights = jnp.exp2((score_ref[chunk_rows, lanes] - row_top[c]) * score_unit)
            sums[c] = sums[c] + fold_rows(weights, jnp.sum)
            total_ref[:, lanes] += dot_00(values, weights.astype(jnp.bfloat16))
        return tuple(sums)

    sums = lax.fori_loop(
        first_chunk, past_chunk, value_step, tuple((jnp.zeros((8, wide), jnp.float32) for _ in range(3)))
    )
    for c in range(3):
        row_sum = jnp.sum(sums[c], axis=0, keepdims=True)
        mixed = total_ref[:, c * wide : (c + 1) * wide]
        if is_self and c > 0:
            own_weight = jnp.exp2((own_score[c] - row_top[c]) * score_unit)
            row_sum = row_sum + own_weight
            value_turned = turned_twice(vo_ref[0, c - 1])
            mixed = mixed + own_weight * value_turned
        mixed = mixed / row_sum
        o_ref[0, c] = join_heads(mixed.T, half).astype(jnp.bfloat16)
        lse_ref[0, 0, :, c * wide : (c + 1) * wide] = row_top[c] * score_unit + jnp.log2(row_sum)


def backward_kernel(is_self, rows, near_tiles, *refs):
    if is_self:
        (bounds_ref, q_ref, k_ref, v_ref, o_ref, do_ref, lse_ref, ko_ref, vo_ref, bias_ref, own_bias_ref,
         dq_ref, dk_ref, dv_ref, dko_ref, dvo_ref, tiles_ref, own_sum_ref, prob_ref, grad_ref, total_ref) = refs
    else:
        (bounds_ref, q_ref, k_ref, v_ref, o_ref, do_ref, lse_ref,
         dq_ref, dk_ref, dv_ref, prob_ref, grad_ref, total_ref) = refs
    stream = pl.program_id(1)
    half = q_ref.shape[3] // 2
    wide = 2 * rows
    first_chunk = bounds_ref[stream, 0] // 2
    past_chunk = bounds_ref[stream, 1] // 2 + 1
    place, blocks = bounds_ref[stream, 2], k_ref.shape[0]
    chunk_count = blocks // 2
    q_tall = [two_heads(q_ref[0, c], half) for c in range(3)]
    do_tall = [two_heads(do_ref[0, c], half) for c in range(3)]
    q_turned = [tall.T for tall in q_tall]
    do_turned = [tall.T for tall in do_tall]
    lse = [lse_ref[0, 0, :, c * wide : (c + 1) * wide] for c in range(3)]
    centre = []
    for c in range(3):
        o_turned = turned_twice(o_ref[0, c])
        centre.append(jnp.sum(do_turned[c].astype(jnp.float32) * o_turned, axis=0, keepdims=True))
    q_all = jnp.concatenate(q_tall, axis=0)
    do_all = jnp.concatenate(do_tall, axis=0)
    total_ref[...] = jnp.zeros_like(total_ref)

    if is_self:

        @pl.when(stream == 0)
        def _():
            tiles_ref[...] = jnp.zeros_like(tiles_ref)
            own_sum_ref[...] = jnp.zeros_like(own_sum_ref)

    def blank_step(chunk, carry):
        for part in range(2):
            slot = slot_of(place, 2 * chunk + part, blocks)
            dk_ref[slot, 0] = jnp.zeros((rows, 2 * half), jnp.bfloat16)
            dv_ref[slot, 0] = jnp.zeros((rows, 2 * half), jnp.bfloat16)
        return carry

    lax.fori_loop(0, first_chunk, blank_step, 0)
    lax.fori_loop(past_chunk, chunk_count, blank_step, 0)

    def chunk_step(chunk, carry):
        for part in range(2):
            block = 2 * chunk + part
            part_rows = pl.ds(part * rows, rows)
            keys = k_ref[slot_of(place, block, blocks), 0]
            values = v_ref[slot_of(place, block, blocks), 0]
            if is_self:
                diag_tile, plain_tile = tile_of(bounds_ref, stream, block, near_tiles)
                later_tile = jnp.where(diag_tile == 0, 1, plain_tile)
                tile_index = (jnp.where(diag_tile == 0, 0, plain_tile), later_tile, later_tile)
            grad_sum = None
            for c in range(3):
                lanes = pl.ds(c * wide, wide)
                scores = dot_10(keys, q_turned[c])
                if is_self:
                    scores = scores + bias_ref[0, tile_index[c]]
                else:
                    scores = scores + shift_of(bounds_ref, stream, block)
                probs = jnp.exp2(scores * score_unit - lse[c])
                prob_ref[part_rows, lanes] = probs.astype(jnp.bfloat16)
                grads = probs * (dot_10(values, do_turned[c]) - centre[c])
                grad_ref[part_rows, lanes] = grads.astype(jnp.bfloat16)
                if is_self:
                    grad_sum = grads if grad_sum is None else grad_sum + grads
            if is_self:
                tiles_ref[0, tile_index[1]] += grad_sum
        slots = [slot_of(place, 2 * chunk + part, blocks) for part in range(2)]
        value_grads = dot_10(prob_ref[...], do_all).astype(jnp.bfloat16)
        key_grads = (0.125 * dot_10(grad_ref[...], q_all)).astype(jnp.bfloat16)
        for part in range(2):
            dv_ref[slots[part], 0] = value_grads[part * rows : (part + 1) * rows]
            dk_ref[slots[part], 0] = key_grads[part * rows : (part + 1) * rows]
        total_ref[...] += dot_00(jnp.concatenate([k_ref[slot, 0] for slot in slots], axis=0), grad_ref[...])
        return carry

    lax.fori_loop(first_chunk, past_chunk, chunk_step, 0)
    for c in range(3):
        turned = total_ref[:, c * wide : (c + 1) * wide]
        if is_self and c > 0:
            own_turned = turned_twice(ko_ref[0, c - 1])
            value_turned = turned_twice(vo_ref[0, c - 1])
            q_wide = q_turned[c].astype(jnp.float32)
            do_wide = do_turned[c].astype(jnp.float32)
            own_score = jnp.sum(q_wide * own_turned, axis=0, keepdims=True) + own_bias_ref[0]
            own_prob = jnp.exp2(own_score * score_unit - lse[c])
            own_dp = jnp.sum(do_wide * value_turned, axis=0, keepdims=True)
            own_grad = own_prob * (own_dp - centre[c])
            own_sum_ref[0] += own_grad
            own_grad = own_grad.astype(jnp.bfloat16).astype(jnp.float32)
            own_low = own_prob.astype(jnp.bfloat16).astype(jnp.float32)
            turned = turned + own_grad * own_turned
            dko = (0.125 * own_grad * q_wide).T
            dko_ref[0, c - 1] = (dko[:rows] + dko[rows:]).astype(jnp.bfloat16)
            dvo = (own_low * do_wide).T
            dvo_ref[0, c - 1] = (dvo[:rows] + dvo[rows:]).astype(jnp.bfloat16)
        dq_ref[0, c] = (0.125 * join_heads(turned.T, half)).astype(jnp.bfloat16)


def attend_forward(bounds, query, keys, values, own=None, near_tiles=0, head_size=64):
    streams, _, rows, width = query.shape
    blocks = keys.shape[0]
    length = blocks * rows
    lanes = 2 * head_size
    pairs = width // lanes
    is_self = own is not None
    row_spec = pl.BlockSpec((1, 3, rows, lanes), lambda p, n, s: (n, 0, 0, p))
    key_spec = pl.BlockSpec((blocks, 1, rows, lanes), lambda p, n, s: (0, n, 0, p))
    in_specs = [row_spec, key_spec, key_spec]
    args = [query, keys, values]
    if is_self:
        own_keys, own_values, tiles, own_bias = own
        own_spec = pl.BlockSpec((1, 2, rows, lanes), lambda p, n, s: (n, 0, 0, p))
        in_specs += [
            own_spec,
            own_spec,
            pl.BlockSpec((1,) + tiles.shape[1:], lambda p, n, s: (p, 0, 0, 0)),
            pl.BlockSpec((1, 1, 2 * rows), lambda p, n, s: (p, 0, 0)),
        ]
        args += [own_keys, own_values, tiles, own_bias]
    return pl.pallas_call(
        partial(forward_kernel, is_self, rows, near_tiles),
        grid_spec=pltpu.PrefetchScalarGridSpec(
            num_scalar_prefetch=1,
            grid=(pairs, streams),
            in_specs=in_specs,
            out_specs=[row_spec, pl.BlockSpec((1, 1, 1, 6 * rows), lambda p, n, s: (p, n, 0, 0))],
            scratch_shapes=[
                pltpu.VMEM((length, 6 * rows), jnp.float32),
                pltpu.VMEM((lanes, 6 * rows), jnp.float32),
            ],
        ),
        out_shape=[
            jax.ShapeDtypeStruct(query.shape, jnp.bfloat16),
            jax.ShapeDtypeStruct((pairs, streams, 1, 6 * rows), jnp.float32),
        ],
        compiler_params=pltpu.CompilerParams(vmem_limit_bytes=20 * 1024 * 1024),
        cost_estimate=pl.CostEstimate(flops=0, bytes_accessed=0, transcendentals=0),
    )(bounds, *args)


def attend_backward(bounds, query, keys, values, mixed, mix_grad, lse, own=None, near_tiles=0, head_size=64):
    streams, _, rows, width = query.shape
    blocks = keys.shape[0]
    length = blocks * rows
    lanes = 2 * head_size
    pairs = width // lanes
    is_self = own is not None
    row_spec = pl.BlockSpec((1, 3, rows, lanes), lambda p, n, s: (n, 0, 0, p))
    key_spec = pl.BlockSpec((blocks, 1, rows, lanes), lambda p, n, s: (0, n, 0, p))
    in_specs = [row_spec, key_spec, key_spec, row_spec, row_spec,
                pl.BlockSpec((1, 1, 1, 6 * rows), lambda p, n, s: (p, n, 0, 0))]
    args = [query, keys, values, mixed, mix_grad, lse]
    out_specs = [row_spec, key_spec, key_spec]
    out_shape = [jax.ShapeDtypeStruct(query.shape, jnp.bfloat16)] + [jax.ShapeDtypeStruct(keys.shape, jnp.bfloat16)] * 2
    if is_self:
        own_keys, own_values, tiles, own_bias = own
        own_spec = pl.BlockSpec((1, 2, rows, lanes), lambda p, n, s: (n, 0, 0, p))
        tile_spec = pl.BlockSpec((1,) + tiles.shape[1:], lambda p, n, s: (p, 0, 0, 0))
        own_bias_spec = pl.BlockSpec((1, 1, 2 * rows), lambda p, n, s: (p, 0, 0))
        in_specs += [own_spec, own_spec, tile_spec, own_bias_spec]
        args += [own_keys, own_values, tiles, own_bias]
        out_specs += [own_spec, own_spec, tile_spec, own_bias_spec]
        out_shape += [jax.ShapeDtypeStruct(own_keys.shape, jnp.bfloat16)] * 2
        out_shape += [jax.ShapeDtypeStruct(tiles.shape, jnp.float32), jax.ShapeDtypeStruct(own_bias.shape, jnp.float32)]
    return pl.pallas_call(
        partial(backward_kernel, is_self, rows, near_tiles),
        grid_spec=pltpu.PrefetchScalarGridSpec(
            num_scalar_prefetch=1,
            grid=(pairs, streams),
            in_specs=in_specs,
            out_specs=out_specs,
            scratch_shapes=[
                pltpu.VMEM((2 * rows, 6 * rows), jnp.bfloat16),
                pltpu.VMEM((2 * rows, 6 * rows), jnp.bfloat16),
                pltpu.VMEM((lanes, 6 * rows), jnp.float32),
            ],
        ),
        out_shape=out_shape,
        compiler_params=pltpu.CompilerParams(vmem_limit_bytes=20 * 1024 * 1024),
        cost_estimate=pl.CostEstimate(flops=0, bytes_accessed=0, transcendentals=0),
    )(bounds, *args)


def bucket_of(distance):
    nearby = jnp.maximum(distance, 0)
    distant = 16 + sum(((nearby >= edge).astype(jnp.int32) for edge in bucket_edges))
    return jnp.where(nearby < 16, nearby, distant)


def near_count(rows):
    gap = 1
    while rows * gap - (rows - 1) < bucket_edges[-1]:
        gap += 1
    return gap


def bias_tiles(rel_table, rows):
    heads, buckets = rel_table.shape
    near_tiles = near_count(rows)
    places = jnp.arange(rows, dtype=jnp.int32)
    distance = places[None, None, :] - places[None, :, None] + rows * jnp.arange(near_tiles, dtype=jnp.int32)[:, None, None]
    onehot = (bucket_of(distance)[..., None] == jnp.arange(buckets, dtype=jnp.int32)).astype(jnp.float32)
    shifted = 8.0 * (rel_table - rel_table[:, buckets - 1 :])
    gap = jnp.tile(places[None, :] - places[:, None], (1, 2))[None, None]
    near = jnp.concatenate(
        [
            jnp.einsum("dstk,pk->pdst", onehot, shifted[side::2], precision=lax.Precision.HIGHEST)
            for side in range(2)
        ],
        axis=-1,
    )
    diag = near[:, :1]
    tiles = jnp.concatenate(
        [
            jnp.where(gap >= 0, diag, masked_out),
            jnp.where(gap > 0, diag, masked_out),
            near[:, 1:],
            jnp.zeros_like(diag),
            jnp.full_like(diag, masked_out),
        ],
        axis=1,
    )
    own_bias = jnp.repeat(shifted[:, 0], rows).reshape(heads // 2, 1, 2 * rows)
    return tiles, own_bias, onehot


def table_grad(tile_grads, own_sums, onehot, bucket_count):
    pairs, tile_count, rows, wide = tile_grads.shape
    near_tiles = tile_count - 3
    sides = (tile_grads[..., : wide // 2], tile_grads[..., wide // 2 :])
    near_part, far_part = (
        jnp.stack(parts, axis=1)
        for parts in zip(
            *(
                (
                    jnp.einsum(
                        "pdst,dstk->pk", side[:, 1 : 1 + near_tiles], onehot, precision=lax.Precision.HIGHEST
                    ),
                    jnp.sum(side[:, 1 + near_tiles], axis=(1, 2)),
                )
                for side in sides
            )
        )
    )
    own_part = jnp.sum(own_sums.reshape(pairs, 2, wide // 2), axis=-1)
    buckets = jnp.arange(bucket_count)
    result = near_part + far_part[..., None] * (buckets == bucket_count - 1) + own_part[..., None] * (buckets == 0)
    return result.reshape(2 * pairs, bucket_count)


def norm_parts(values_in):
    centred = values_in - jnp.mean(values_in, axis=-1, keepdims=True)
    inv_scale = lax.rsqrt(jnp.mean(centred * centred, axis=-1, keepdims=True) + 1e-05)
    return (centred * inv_scale, inv_scale)


def norm_back(grad_in, normed, inv_scale, gain_row):
    scaled = grad_in * gain_row
    return inv_scale * (
        scaled
        - jnp.mean(scaled, axis=-1, keepdims=True)
        - normed * jnp.mean(scaled * normed, axis=-1, keepdims=True)
    )


def matmul(left_side, right_side):
    return jnp.einsum("...i,ij->...j", left_side, right_side, preferred_element_type=jnp.float32)


def matmul_t(left_side, right_side):
    return jnp.einsum("...j,ij->...i", left_side, right_side, preferred_element_type=jnp.float32)


def swap_core(values_in):
    size = lax.axis_size("dp")
    return lax.ppermute(values_in, "dp", [(i, i ^ 1) for i in range(size)])


def swap_chip(values_in):
    size = lax.axis_size("dp")
    return lax.ppermute(values_in, "dp", [(i, i ^ 2) for i in range(size)])


def swap_block(values_in, bit):
    size = lax.axis_size("blk")
    return lax.ppermute(values_in, "blk", [(i, i ^ bit) for i in range(size)])


def tie(value, *earlier):
    return lax.optimization_barrier((value,) + earlier)[0]


def assemble(pieces):
    count = pieces[0].shape[0]

    def ordered(at):
        def joined(*parts):
            return [jnp.concatenate([parts[at ^ index][k] for index in range(4)], axis=0) for k in range(count)]

        return joined

    return lax.switch(lax.axis_index("dp"), [ordered(at) for at in range(4)], *pieces)


def outer_low(left_side, right_side):
    return jnp.einsum("ni,nj->ij", left_side, right_side, preferred_element_type=jnp.float32)


def pick(values_in, index, axis):
    return lax.dynamic_index_in_dim(values_in, index, axis, keepdims=False)


def add_low(kept, arrived):
    return (kept.astype(jnp.float32) + arrived.astype(jnp.float32)).astype(jnp.bfloat16)


def open_core(grads):
    core = lax.axis_index("dp") % 2
    blocks = lax.axis_size("blk")

    def split(core_at):
        return jnp.stack(
            [pick(g.reshape(2, 2, blocks, g.shape[0] // (4 * blocks), g.shape[1]), core_at, 1) for g in grads], axis=2
        )

    return split(1 - core), split(core)


def open_chip(values_in):
    chip = lax.axis_index("dp") // 2
    return pick(values_in, 1 - chip, 0), pick(values_in, chip, 0)


def open_block(values_in, axis, bit):
    shape = values_in.shape
    values_in = values_in.reshape(shape[:axis] + (shape[axis] // 2, 2) + shape[axis + 1 :])
    mine = (lax.axis_index("blk") // bit) % 2
    return pick(values_in, 1 - mine, axis + 1), pick(values_in, mine, axis + 1)


def gather_far_first(values_in):
    even = [values_in]
    odd = [swap_block(values_in, 1)]
    before = values_in
    for gap in range(2, lax.axis_size("blk"), 2):
        piece = swap_block(values_in if gap <= 4 else tie(values_in, before), gap)
        before = piece
        even.append(piece)
        odd.append(swap_block(piece, 1))
    return jnp.stack(even + odd), before


def gather_near_first(values_in, *earlier):
    both = jnp.stack([values_in, swap_block(values_in, 1)])
    sent = tie(both, *earlier)
    pieces = [both] + [swap_block(sent, gap) for gap in range(2, lax.axis_size("blk"), 2)]
    return jnp.stack(pieces, axis=1).reshape((lax.axis_size("blk"),) + values_in.shape)


def fold_odd(terms):
    half = terms.shape[0] // 2
    return terms[:half], swap_block(terms[half:], 1)


def fold_even(terms):
    return sum(
        [swap_block(terms[index], 2 * index).astype(jnp.float32) for index in range(1, terms.shape[0])],
        terms[0].astype(jnp.float32),
    )


def fold_far_first(terms):
    half = terms.shape[0] // 2
    split = terms.reshape((2, half) + terms.shape[1:])
    return split[:, 0], [swap_block(split[:, index], 2 * index) for index in range(1, half)]


def sum_all(kept, come):
    return sum([piece.astype(jnp.float32) for piece in come], kept.astype(jnp.float32))


def start_exchange(values_in):
    mine = lax.axis_index("blk") // 2
    come = [swap_block(pick(values_in, mine ^ gap, 0), 2 * gap) for gap in range(1, values_in.shape[0])]
    return pick(values_in, mine, 0), come


def split_shares(share):
    share = share.astype(jnp.float32)
    return [share[k] for k in range(share.shape[0])]


def sum_everywhere(values_in):
    blocks = lax.axis_size("blk")
    mine = lax.axis_index("blk") // 2
    come = jnp.stack([values_in] + [swap_block(values_in, 2 * gap) for gap in range(1, blocks // 2)])
    total = sum(pick(come, mine ^ index, 0) for index in range(blocks // 2))
    total = total + swap_core(total)
    total = total + swap_block(total, 1)
    return total + swap_chip(total)


def shards(
    hidden,
    encoder,
    lengths,
    qkv_self,
    out_self,
    rel_table,
    qkv_cross,
    out_cross,
    ffn_in,
    ffn_out,
    norm_gain,
    norm_bias,
    cotangent,
):
    streams, _, rows, width = hidden.shape
    heads, buckets = rel_table.shape
    head_size = width // heads
    place = lax.axis_index("blk")
    main_all, main_last = gather_far_first(hidden[:, 0])
    enc_all = gather_near_first(encoder, main_last)
    low = partial(lax.convert_element_type, new_dtype=jnp.bfloat16)
    qkv_low = low(qkv_self)
    middle_low = jnp.concatenate([low(out_self)[None], low(qkv_cross), low(out_cross)[None]])
    first_low_w, second_low_w = low(ffn_in)[None], low(ffn_out)[None]
    qkv_far = swap_chip(qkv_low)
    w_qkv = assemble([qkv_low, swap_core(qkv_low), qkv_far, swap_core(qkv_far)])
    doc_ends = jnp.cumsum(lengths, axis=-1)
    begin = place * rows
    doc_begin = jnp.max(jnp.where(doc_ends <= begin, doc_ends, 0), axis=-1)
    doc_end = jnp.min(jnp.where(doc_ends > begin, doc_ends, rows * lax.axis_size("blk")), axis=-1)
    first_block = (doc_begin // rows).astype(jnp.int32)
    last_block = (doc_end // rows - 1).astype(jnp.int32)
    places = jnp.full_like(first_block, place)
    self_bounds = jnp.stack([first_block, places, places], axis=1)
    cross_bounds = jnp.stack([first_block, last_block, places], axis=1)
    near_tiles = near_count(rows)
    tiles, own_bias, onehot = bias_tiles(rel_table, rows)

    def flat(values_in):
        return values_in.reshape(-1, values_in.shape[-1])

    def tall(values_in):
        return values_in.reshape(streams, 3, rows, width)

    hidden_own = hidden[:, 1:]
    query = matmul(hidden, w_qkv[0]).astype(jnp.bfloat16)
    own_keys = matmul(hidden_own, w_qkv[1]).astype(jnp.bfloat16)
    own_values = matmul(hidden_own, w_qkv[2]).astype(jnp.bfloat16)
    middle_far = swap_chip(tie(middle_low, qkv_far))
    main_keys = matmul(main_all, w_qkv[1]).astype(jnp.bfloat16)
    main_values = matmul(main_all, w_qkv[2]).astype(jnp.bfloat16)
    own = (own_keys, own_values, tiles, own_bias)

    first_far = swap_chip(tie(first_low_w, main_values, query))
    attended, self_lse = attend_forward(
        self_bounds, query, main_keys, main_values, own, near_tiles, head_size
    )
    second_far = swap_chip(tie(second_low_w, first_far))
    middle_pieces = [middle_low, swap_core(middle_low), middle_far, swap_core(tie(middle_far, attended))]
    w_out, *c_qkv, c_out = assemble(middle_pieces)
    first_norm, first_scale = norm_parts(
        flat(hidden).astype(jnp.float32) + matmul(flat(attended), w_out)
    )
    first_out = first_norm * norm_gain[0] + norm_bias[0]
    first_low = first_out.astype(jnp.bfloat16)
    cross_query = matmul(first_low, c_qkv[0]).astype(jnp.bfloat16)
    enc_keys = matmul(enc_all, c_qkv[1]).astype(jnp.bfloat16)
    enc_values = matmul(enc_all, c_qkv[2]).astype(jnp.bfloat16)
    cross_att, cross_lse = attend_forward(
        cross_bounds, tall(cross_query), enc_keys, enc_values, None, 0, head_size
    )
    w_first, w_second = (
        assemble([shard, swap_core(shard), far, swap_core(far)])[0]
        for shard, far in ((first_low_w, tie(first_far, cross_query)), (second_low_w, tie(second_far, cross_query)))
    )
    second_norm, second_scale = norm_parts(first_out + matmul(flat(cross_att), c_out))
    second_out = second_norm * norm_gain[1] + norm_bias[1]
    second_low = second_out.astype(jnp.bfloat16)
    inner_act = matmul(second_low, w_first)
    normal_cdf = 0.5 * (1.0 + lax.erf(inner_act * math.sqrt(0.5)))
    activated = (inner_act * normal_cdf).astype(jnp.bfloat16)
    density = jnp.exp(-0.5 * inner_act * inner_act) * (1.0 / math.sqrt(2.0 * math.pi))
    act_slope = (normal_cdf + inner_act * density).astype(jnp.bfloat16)
    third_norm, third_scale = norm_parts(second_out + matmul(activated, w_second))
    output = tall((third_norm * norm_gain[2] + norm_bias[2]).astype(jnp.bfloat16))

    grad_out = flat(cotangent).astype(jnp.float32)
    gain_three = jnp.sum(grad_out * third_norm, axis=0)
    bias_three = jnp.sum(grad_out, axis=0)
    third_grad = norm_back(grad_out, third_norm, third_scale, norm_gain[2])
    third_low = third_grad.astype(jnp.bfloat16)
    second_part = outer_low(activated, third_low).astype(jnp.bfloat16)
    second_sent, second_kept = open_core([second_part])
    second_come = swap_core(second_sent)
    inner_grad = (
        matmul_t(tie(third_low, second_sent), w_second) * act_slope.astype(jnp.float32)
    ).astype(jnp.bfloat16)
    row_sent, row_kept = open_block(add_low(second_kept, second_come), 1, 1)
    row_come = swap_block(row_sent, 1)
    inner_grad = tie(inner_grad, row_sent)
    first_part = outer_low(second_low, inner_grad).astype(jnp.bfloat16)
    first_sent, first_kept = open_core([first_part])
    first_come = swap_core(first_sent)
    second_total = third_grad + matmul_t(tie(inner_grad, first_sent), w_first)
    gain_two = jnp.sum(second_total * second_norm, axis=0)
    bias_two = jnp.sum(second_total, axis=0)
    second_grad = norm_back(second_total, second_norm, second_scale, norm_gain[1])
    cross_low = second_grad.astype(jnp.bfloat16)
    first_chip_sent, first_chip_kept = open_chip(add_low(first_kept, first_come))
    first_chip_come = swap_chip(first_chip_sent)
    cross_mix_grad = tall(matmul_t(tie(cross_low, first_chip_sent), c_out).astype(jnp.bfloat16))
    cross_query_grad, enc_key_grad, enc_value_grad = attend_backward(
        cross_bounds, tall(cross_query), enc_keys, enc_values, cross_att, cross_mix_grad, cross_lse,
        None, 0, head_size,
    )
    chip_sent, chip_kept = open_chip(add_low(row_kept, tie(row_come, enc_key_grad)))
    chip_come = swap_chip(chip_sent)
    enc_key_grad = tie(enc_key_grad, chip_sent)
    encoder_terms = (matmul_t(enc_key_grad, c_qkv[1]) + matmul_t(enc_value_grad, c_qkv[2])).astype(jnp.bfloat16)
    encoder_kept, encoder_come = fold_far_first(encoder_terms)
    first_row_sent, first_row_kept = open_block(add_low(first_chip_kept, tie(first_chip_come, encoder_terms)), 0, 1)
    first_row_come = swap_block(first_row_sent, 1)
    first_total = second_grad + matmul_t(flat(tie(cross_query_grad, first_row_sent)), c_qkv[0])
    gain_one = jnp.sum(first_total * first_norm, axis=0)
    bias_one = jnp.sum(first_total, axis=0)
    first_grad = norm_back(first_total, first_norm, first_scale, norm_gain[0])
    out_low = first_grad.astype(jnp.bfloat16)
    cross_parts = [
        outer_low(flat(left), flat(right)).astype(jnp.bfloat16)
        for left, right in (
            (cross_att, cross_low),
            (first_low, cross_query_grad),
            (enc_all, tie(enc_key_grad, out_low)),
            (enc_all, enc_value_grad),
            (attended, out_low),
        )
    ]
    cross_sent, cross_kept = open_core(cross_parts)
    cross_come = swap_core(cross_sent)
    mix_grad = tall(matmul_t(tie(out_low, cross_sent), w_out).astype(jnp.bfloat16))
    cross_chip_sent, cross_chip_kept = open_chip(add_low(cross_kept, tie(cross_come, mix_grad)))
    cross_chip_come = swap_chip(cross_chip_sent)
    second_half = add_low(chip_kept, tie(chip_come, mix_grad))
    g_second = sum_all(*start_exchange(second_half))[0]
    mix_grad = tie(mix_grad, cross_chip_sent, second_half)
    query_grad, key_grad, value_grad, own_key_grad, own_value_grad, tile_grads, own_sums = attend_backward(
        self_bounds, query, main_keys, main_values, attended, mix_grad, self_lse, own, near_tiles, head_size
    )
    first_half = add_low(first_row_kept, tie(first_row_come, query_grad))
    g_first = sum_all(*start_exchange(first_half))[0]
    key_grad = tie(key_grad, first_half)
    main_terms = (matmul_t(key_grad, w_qkv[1]) + matmul_t(value_grad, w_qkv[2])).astype(jnp.bfloat16)
    main_kept, main_come = fold_odd(main_terms)
    main_come_from = main_terms
    encoder_half = sum_all(encoder_kept, [tie(piece, main_terms) for piece in encoder_come]).astype(jnp.bfloat16)
    d_encoder = sum_all(encoder_half[0], [swap_block(encoder_half[1], 1)])
    own_flat = flat(hidden_own)
    main_flat = flat(main_all)
    started = tie(query_grad, main_come_from, encoder_half)
    self_parts = [outer_low(flat(hidden), flat(started)).astype(jnp.bfloat16)] + [
        (outer_low(main_flat, flat(tie(grad, started))) + outer_low(own_flat, flat(own_grad))).astype(jnp.bfloat16)
        for grad, own_grad in ((key_grad, own_key_grad), (value_grad, own_value_grad))
    ]
    self_sent, self_kept = open_core(self_parts)
    self_come = swap_core(self_sent)
    local_grad = tall(first_grad) + matmul_t(tie(query_grad, self_sent), w_qkv[0])
    self_chip_sent, self_chip_kept = open_chip(add_low(self_kept, tie(self_come, local_grad)))
    self_chip_come = swap_chip(self_chip_sent)
    own_back = matmul_t(tie(own_key_grad, self_chip_sent), w_qkv[1]) + matmul_t(own_value_grad, w_qkv[2])
    main_half = add_low(main_kept, tie(main_come, own_back))
    main_back = fold_even(main_half)
    cross_half = add_low(cross_chip_kept, tie(cross_chip_come, main_half))
    late_sent, late_kept = open_block(
        jnp.concatenate([cross_half, add_low(self_chip_kept, tie(self_chip_come, main_half))], axis=1), 0, 1
    )
    late_half = add_low(late_kept, swap_block(late_sent, 1))
    late_share = sum_all(*start_exchange(late_half))
    g_cross_out, *g_cross, g_self_out = split_shares(late_share[:5])
    g_cross = jnp.stack(g_cross)
    g_qkv = late_share[5:]
    d_hidden = local_grad + jnp.concatenate([main_back[:, None], own_back], axis=1)
    rel_grad = table_grad(tile_grads, own_sums, onehot, buckets)
    small = jnp.concatenate(
        [
            jnp.stack([gain_one, gain_two, gain_three, bias_one, bias_two, bias_three]),
            rel_grad.reshape(-1, width) if rel_grad.size % width == 0 else
            jnp.pad(rel_grad.reshape(1, -1), ((0, 0), (0, width - rel_grad.size))),
        ]
    )
    small = sum_everywhere(small)
    return (
        output,
        d_hidden,
        d_encoder,
        g_qkv,
        g_self_out,
        small[6:].reshape(-1)[: heads * buckets].reshape(heads, buckets),
        g_cross,
        g_cross_out,
        g_first,
        g_second,
        small[0:3],
        small[3:6],
    )


def solution(mesh):
    in_specs = (
        P("dp", None, "blk", None),
        P("dp", "blk", None),
        P("dp", None),
        P(None, "dp", None),
        P("dp", None),
        P(),
        P(None, "dp", None),
        P("dp", None),
        P("dp", None),
        P("dp", None),
        P(),
        P(),
        P("dp", None, "blk", None),
    )
    out_specs = (
        P("dp", None, "blk", None),
        P("dp", None, "blk", None),
        P("dp", "blk", None),
        P(None, ("dp", "blk"), None),
        P(("dp", "blk"), None),
        P(),
        P(None, ("dp", "blk"), None),
        P(("dp", "blk"), None),
        P(("dp", "blk"), None),
        P(("dp", "blk"), None),
        P(),
        P(),
    )
    return jax.shard_map(shards, mesh=mesh, in_specs=in_specs, out_specs=out_specs, check_vma=False)
```
